256 devices in a mesh: dp: 128 (over y_hi, z, x, core), mp: 2 (over y_lo).
Axes of the slice: x: 4, y: 4 (y_hi: 2, y_lo: 2; y = y_hi * 2 + y_lo), z: 8, core: 2. Of those that a mesh axis runs over, the one named last changes fastest.
Arguments:
- query_hidden: bfloat16 [1024, 4096], P('dp', 'mp'), may hold values from -0.119628906 to 0.119628906
- passage_hidden: bfloat16 [1024, 4096], P('dp', 'mp'), may hold values from -0.119628906 to 0.119628906
- hard_hidden: bfloat16 [65536, 4096], P('dp', 'mp'), may hold values from -0.119628906 to 0.119628906
- gain: float32 [4096], P('mp'), may hold values from 0.5 to 1.5
- hard_owner: int32 [1024, 31, 1], P('dp'), may hold values from 0 to 127; in each aligned block of 248 rows (0 to 247, 248 to 495, ..., all dimensions but the last counted through in order) at most 3 rows name the same one
- hard_slot: int32 [1024, 31], P('dp'), may hold values from 0 to 511
Outputs:
- grad_query_hidden: bfloat16 [1024, 4096], P('dp', 'mp')
- grad_passage_hidden: bfloat16 [1024, 4096], P('dp', 'mp')
- grad_hard_hidden: bfloat16 [65536, 4096], P('dp', 'mp')
- grad_gain: float32 [4096], P('mp')
- loss: float32 [], replicated
The draws below stay inside these ranges and needn't reach their ends.
Inputs may be any that keep to these rules, and one draw needn't show every extreme that they name: `hard_owner`: among the 248 hard negatives of the queries of one index of dp, no owner is named more than 3 times, a bound that some block reaches.
All inputs are finite; a program needn't handle non-finite values.
Results may differ from the reference program's by a relative error of at most 0.01105.
Values may be sent and summed in bfloat16 or wider, within the bound.
No kernel may reach another device: no remote copies, remote signals or barrier semaphores. Data moves between devices by JAX's collectives and lax.ppermute only.
A program may use at most 64 MiB of HBM per device.

```python
import math
import jax
import jax.numpy as jnp
import numpy as np
from jax import lax

D = 4096
QD = 8
DIFFICULT_FOILS = 31
HP_DEV = 512
CAP = 3
Q = 1024
NP = 65536
N_DP = 128


def place_ends(result, stream_key, low, largest):
    index_at = [jax.random.randint(jax.random.fold_in(stream_key, axis), (), 0, length) for axis, length in enumerate(result.shape)]
    main_axis = result.shape.index(max(result.shape))
    neighbour = index_at[:main_axis] + [(index_at[main_axis] + 1) % result.shape[main_axis]] + index_at[main_axis + 1:]
    return result.at[tuple(index_at)].set(low).at[tuple(neighbour)].set(largest)


def shard_levels(key, extent, cuts, least, high):
    def one(dim, blocks):
        steps = jax.random.uniform(jax.random.fold_in(jax.random.fold_in(key, 6), dim), (blocks,), jnp.float32, least / len(cuts), high / len(cuts))
        return jnp.repeat(jnp.exp(steps), extent[dim] // blocks).reshape((-1,) + (1,) * (len(extent) - dim - 1))

    factor_of = one(*cuts[0])
    for cut in cuts[1:]:
        factor_of = factor_of * one(*cut)
    return factor_of


def routed_block(key, own, number, rows, number_of, top, bound, lean):
    ranking = jax.random.permutation(key, number_of)
    heavy_load, usual = portions_of(number_of, rows * top, bound, lean, True), portions_of(number_of, rows * top, bound, lean, False)
    places = jnp.arange(number_of)

    def named(tallies, turn):
        used = int((tallies > 0).sum())
        fixed = max(1, used // 4)
        passed = fixed + (places - fixed + turn * (used - fixed)) % max(1, number_of - fixed)
        return jnp.zeros((number_of,), jnp.int32).at[ranking[jnp.where(places < fixed, places, passed)]].set(jnp.asarray(tallies, jnp.int32))

    tallies = jnp.where(number % 4 == 0, named(heavy_load, number // 4), named(usual, number - number // 4 - 1))
    mixed = jax.random.permutation(jax.random.fold_in(own, 3), number_of)
    giver, receiver = mixed[0:number_of // 2 * 2:2], mixed[1:number_of // 2 * 2:2]
    room = jnp.minimum(tallies[giver] - 1, bound - tallies[receiver]) // 2
    room = jnp.where((giver == ranking[0]) | (receiver == ranking[0]) | (tallies[receiver] == 0), 0, jnp.maximum(room, 0))
    passed = jax.random.randint(jax.random.fold_in(own, 4), (number_of // 2,), 0, 1 << 20) % (room + 1)
    tallies = tallies.at[giver].add(-passed).at[receiver].add(passed)
    items = jnp.searchsorted(jnp.cumsum(tallies), jnp.arange(rows * top), side="right").astype(jnp.int32)
    grid = items.reshape(top, rows).T
    grid = grid[jax.random.permutation(jax.random.fold_in(own, 1), rows)]
    turn = jax.random.randint(jax.random.fold_in(own, 2), (rows, 1), 0, top)
    return jnp.take_along_axis(grid, (jnp.arange(top)[None, :] + turn) % top, axis=1)


def portions_of(number_of, total, reach, slope, full):
    loads = [(1 << 20) // math.isqrt(grade ** slope) + 1 for grade in range(1, number_of + 1)]
    largest = reach if full else min(reach, max(-(-total // number_of), total * loads[0] // sum(loads)))
    least = 1 if total - largest >= number_of - 1 else 0
    given, rest = [largest] + [least] * (number_of - 1), total - largest - least * (number_of - 1)
    while rest > 0:
        movable = [i for i in range(1, number_of) if given[i] < largest] or [i for i in range(1, number_of) if given[i] < reach]
        pool, budget = sum([loads[i] for i in movable]), rest
        for i in movable:
            addition = min(reach - given[i], max(1, budget * loads[i] // pool), rest)
            given[i] = given[i] + addition
            rest = rest - addition
    return np.array(given)


def normal_values(key, dims, spread, bound, split=(), held_as=jnp.bfloat16):
    loudness = shard_levels(key, dims, split, -0.22, 0.18) if split else 1.0
    drawn = jax.random.normal(key, dims, jnp.float32) * spread * loudness
    return jnp.minimum(jnp.maximum(drawn, -bound), bound).astype(held_as)


def setup_inputs(seed: int = 0) -> dict:
    arg_keys = jax.random.split(jax.random.key(seed), 7)
    query_hidden = normal_values(arg_keys[0], (Q, D), 0.02, 0.119628906, ((0, 128), (1, 2)))
    passage_hidden = normal_values(arg_keys[1], (Q, D), 0.02, 0.119628906, ((0, 128), (1, 2)))
    hard_hidden = normal_values(arg_keys[2], (NP, D), 0.02, 0.119628906, ((0, 128), (1, 2)))
    gain = jnp.clip(1.0 + 0.1 * jax.random.normal(arg_keys[3], (D,), jnp.float32), 0.5, 1.5)
    hard_owner_keys = jax.random.split(jax.random.fold_in(arg_keys[4], 1), Q * DIFFICULT_FOILS // (DIFFICULT_FOILS * QD))
    hard_owner_turns = jax.random.permutation(jax.random.fold_in(arg_keys[4], 3), Q * DIFFICULT_FOILS // (DIFFICULT_FOILS * QD))
    hard_owner = jax.vmap(lambda own, number: routed_block(jax.random.fold_in(arg_keys[4], 2), own, number, DIFFICULT_FOILS * QD, N_DP, 1, CAP, 2))(hard_owner_keys, hard_owner_turns).reshape((Q, DIFFICULT_FOILS, 1))
    hard_slot = place_ends(jax.random.randint(arg_keys[5], (Q, DIFFICULT_FOILS), 0, HP_DEV), jax.random.fold_in(arg_keys[5], 1), 0, HP_DEV - 1).astype(jnp.int32)
    return {"query_hidden": query_hidden, "passage_hidden": passage_hidden, "hard_hidden": hard_hidden, "gain": gain, "hard_owner": hard_owner, "hard_slot": hard_slot}


normalizer_divisor = 0.02
eps_norm = 1e-06

def window(hidden, gain):
    values = hidden.astype(jnp.float32)
    scale = lax.rsqrt(lax.optimization_barrier(jnp.mean(values * values, axis=-1, keepdims=True)) + eps_norm)
    scaled = values * scale * gain
    length = jnp.sqrt(lax.optimization_barrier(jnp.sum(scaled * scaled, axis=-1, keepdims=True)) + eps_norm)
    return scaled / length

def window_back(hidden, gain, grad_unit):
    unit, pull_back = jax.vjp(window, hidden.astype(jnp.float32), gain)
    grad_values, grad_gain = pull_back(grad_unit)
    return (grad_values.astype(jnp.bfloat16), grad_gain)

def reference(query_hidden, passage_hidden, hard_hidden, gain, hard_owner, hard_slot):
    overall_aggregate = QD * N_DP
    request_embeddings_list = window(query_hidden, gain).astype(jnp.bfloat16)
    document_embeddings_list = window(passage_hidden, gain).astype(jnp.bfloat16)
    table = hard_hidden.reshape(N_DP, HP_DEV, D)
    emb_h = lax.map(lambda block: window(block, gain).astype(jnp.bfloat16), table).reshape(N_DP * HP_DEV, D)
    ids = (hard_owner[:, :, 0] * HP_DEV + hard_slot).astype(jnp.int32)
    request_tiles = request_embeddings_list.reshape(N_DP, QD, D)
    tile_positions = ids.reshape(N_DP, QD, DIFFICULT_FOILS)

    def difficult_foil_tile(pair):
        request_entries, picks = pair
        near = emb_h[picks].astype(jnp.float32)
        return jnp.einsum('qd,qkd->qk', request_entries.astype(jnp.float32), near)
    difficult_foil_affinity = lax.map(difficult_foil_tile, (request_tiles, tile_positions)).reshape(overall_aggregate, DIFFICULT_FOILS) / normalizer_divisor
    cobatch_raw_affinity = jnp.dot(request_embeddings_list, document_embeddings_list.T, preferred_element_type=jnp.float32) / normalizer_divisor
    highest = jnp.maximum(lax.optimization_barrier(jnp.max(cobatch_raw_affinity, axis=1)), lax.optimization_barrier(jnp.max(difficult_foil_affinity, axis=1)))
    log_total = highest + jnp.log(lax.optimization_barrier(jnp.sum(jnp.exp(cobatch_raw_affinity - highest[:, None]), axis=1)) + lax.optimization_barrier(jnp.sum(jnp.exp(difficult_foil_affinity - highest[:, None]), axis=1)))
    diagonal = jnp.arange(overall_aggregate, dtype=jnp.int32)
    positive = cobatch_raw_affinity[diagonal, diagonal]
    loss = jnp.mean(log_total - positive)
    identity = (diagonal[:, None] == diagonal[None, :]).astype(jnp.float32)
    cobatch_multiplier = (jnp.exp(cobatch_raw_affinity - log_total[:, None]) - identity).astype(jnp.bfloat16)
    coeff_hard = jnp.exp(difficult_foil_affinity - log_total[:, None]).astype(jnp.bfloat16)
    blocks_c = coeff_hard.reshape(N_DP, QD, DIFFICULT_FOILS)

    def hard_pull(pair):
        normalized_probability, picks = pair
        near = emb_h[picks].astype(jnp.float32)
        return jnp.einsum('qk,qkd->qd', normalized_probability.astype(jnp.float32), near)
    difficult_foil_fraction = lax.map(hard_pull, (blocks_c, tile_positions)).reshape(overall_aggregate, D)
    request_embed_derivative = (jnp.dot(cobatch_multiplier, document_embeddings_list, preferred_element_type=jnp.float32) + difficult_foil_fraction) / normalizer_divisor
    document_embed_derivative = jnp.dot(cobatch_multiplier.T, request_embeddings_list, preferred_element_type=jnp.float32) / normalizer_divisor

    def add_block(index, accum):
        normalized_probability = blocks_c[index].astype(jnp.float32)
        request_entries = request_tiles[index].astype(jnp.float32)
        added_portion = normalized_probability[:, :, None] * request_entries[:, None, :] / normalizer_divisor
        return accum.at[tile_positions[index].reshape(-1)].add(added_portion.reshape(-1, D))
    grad_h_emb = lax.fori_loop(0, N_DP, add_block, jnp.zeros((N_DP * HP_DEV, D), jnp.float32))
    grad_q, gain_q = window_back(query_hidden, gain, request_embed_derivative)
    grad_p, gain_p = window_back(passage_hidden, gain, document_embed_derivative)
    grad_h_blocks, gain_h = lax.map(lambda pair: window_back(pair[0], gain, pair[1]), (table, grad_h_emb.reshape(N_DP, HP_DEV, D)))
    grad_h = grad_h_blocks.reshape(N_DP * HP_DEV, D)
    grad_gain = gain_q + gain_p + lax.optimization_barrier(jnp.sum(gain_h, axis=0))
    return (grad_q, grad_p, grad_h, grad_gain, loss)
```

```python
import jax
import jax.numpy as jnp
from jax import lax
from jax.sharding import PartitionSpec as P

D = 4096
normalizer_divisor = 0.02
eps_norm = 1e-06
f32 = jnp.float32
bf16 = jnp.bfloat16
AXES = {"yh": (2, 64), "z": (8, 8), "x": (4, 2), "c": (2, 1)}
SWAP = [(0, 1), (1, 0)]


def shifted(axis, s):
    n, stride = AXES[axis]
    pairs = []
    for i in range(128):
        a = (i // stride) % n
        pairs.append((i, i + ((a + s) % n - a) * stride))
    return pairs


def flipped(bit):
    return [(i, i ^ bit) for i in range(128)]


def gather_axis(x, axis):
    n, _ = AXES[axis]
    parts = [x] + [lax.ppermute(x, "dp", shifted(axis, s)) for s in range(1, n)]
    return jnp.concatenate(parts, 0)


def scatter_axis(x, axis):
    n, _ = AXES[axis]
    rows = x.shape[0] // n
    total = x[:rows].astype(f32)
    for s in range(1, n):
        got = lax.ppermute(x[s * rows : (s + 1) * rows], "dp", shifted(axis, -s))
        total = total + got.astype(f32)
    return total.astype(bf16)


def roll_lanes(v, t):
    return jnp.concatenate([v[:, 128 - t :], v[:, : 128 - t]], 1)


def roll_groups(v, size, t):
    rows = []
    for base in range(0, v.shape[0], size):
        rows += [v[base + size - t : base + size], v[base : base + size - t]]
    return jnp.concatenate(rows, 0)


def sum_relative(v):
    lane = lax.broadcasted_iota(jnp.int32, v.shape, 1)
    got = lax.ppermute(v, "dp", shifted("yh", 1))
    v = v + jnp.where(lane % 16 < 8, roll_lanes(got, 120), roll_lanes(got, 8))
    for t in (1, 2, 4):
        v = v + roll_lanes(lax.ppermute(v, "dp", shifted("z", t)), 16 * t)
    for t in (1, 2):
        v = v + roll_groups(lax.ppermute(v, "dp", shifted("x", t)), 4, t)
    return v + roll_groups(lax.ppermute(v, "dp", shifted("c", 1)), 8, 4)


def sum_all(v):
    for bit in (64, 32, 16, 8, 4, 2, 1):
        v = v + lax.ppermute(v, "dp", flipped(bit))
    return v


def stats(values, gain):
    squares = values * values
    return jnp.sum(squares, axis=1), jnp.sum(squares * gain * gain, axis=1)


def scales(total_sq, total_gsq):
    scale = lax.rsqrt(total_sq / D + eps_norm)
    length = jnp.sqrt(scale * scale * total_gsq + eps_norm)
    return scale, length


def back(values, gain, scale, length, grad_unit, dot):
    ratio = (scale / length)[:, None]
    direct = values * ratio
    grad = ratio * gain * (grad_unit - direct * gain * dot[:, None]) - values * (
        scale * scale * dot * eps_norm / (length * length * D)
    )[:, None]
    return grad.astype(bf16), direct


def local(query_hidden, passage_hidden, hard_hidden, gain, hard_owner, hard_slot):
    me = lax.axis_index("dp")
    inv = 1.0 / normalizer_divisor
    q_vals = query_hidden.astype(f32)
    p_vals = passage_hidden.astype(f32)
    h_vals = hard_hidden.astype(f32)
    mine = jnp.stack(stats(q_vals, gain))
    q_tot = mine + lax.ppermute(mine, "mp", SWAP)
    q_scale, q_length = scales(q_tot[0], q_tot[1])
    q_emb = (q_vals * (q_scale / q_length)[:, None] * gain).astype(bf16)

    owner = hard_owner.reshape(-1)
    slot = hard_slot.reshape(-1)
    count = owner.shape[0]
    number = jnp.arange(count, dtype=jnp.int32)
    earlier = (owner[:, None] == owner[None, :]) & (number[:, None] < number[None, :])
    position = jnp.sum(earlier.astype(jnp.int32), axis=0)
    low = slot % 256
    high = 1 + slot // 256 + 2 * (number // hard_slot.shape[1])
    place = jnp.arange(8, dtype=jnp.int32)[:, None]
    coded = jnp.where(
        place // 2 == position[None, :], jnp.where(place % 2 == 0, low[None, :], high[None, :]), 0
    ).astype(bf16)
    names = (owner[:, None] == jnp.arange(128, dtype=jnp.int32)[None, :]).astype(bf16)
    table = jnp.dot(coded, names, preferred_element_type=f32).astype(bf16)

    panel = jnp.concatenate([q_emb, table], 1)
    for axis in ("yh", "z", "x", "c"):
        panel = gather_axis(panel, axis)
    panel_q = panel[:, :2048]

    p_sq, p_gsq = stats(p_vals, gain)
    h_sq, h_gsq = stats(h_vals, gain)
    mine = jnp.concatenate([p_sq, p_gsq, h_sq, h_gsq])
    tot = mine + lax.ppermute(mine, "mp", SWAP)
    p_scale, p_length = scales(tot[:8], tot[8:16])
    h_scale, h_length = scales(tot[16:528], tot[528:])
    p_emb = (p_vals * (p_scale / p_length)[:, None] * gain).astype(bf16)
    h_emb = (h_vals * (h_scale / h_length)[:, None] * gain).astype(bf16)

    asked = panel[:, 2048:].reshape(128, 8, 128).astype(f32)
    lane = lax.broadcasted_iota(jnp.int32, asked.shape, 2)
    asked = jnp.sum(jnp.where(lane == me, asked, 0.0), axis=2).astype(jnp.int32)
    lows = asked[:, 0:6:2].T.reshape(-1)
    highs = asked[:, 1:6:2].T.reshape(-1)
    valid = highs > 0
    pair_slot = lows + 256 * ((highs - 1) % 2)
    pair_query = (jnp.arange(384, dtype=jnp.int32) % 128) * 8 + (highs - 1) // 2
    pick_q = (pair_query[:, None] == jnp.arange(1024, dtype=jnp.int32)[None, :]) & valid[:, None]
    pick_h = (pair_slot[:, None] == jnp.arange(512, dtype=jnp.int32)[None, :]) & valid[:, None]
    pair_q = jnp.dot(pick_q.astype(bf16), panel_q, preferred_element_type=f32).astype(bf16)
    pair_h = jnp.dot(pick_h.astype(bf16), h_emb, preferred_element_type=f32).astype(bf16)
    part_pair = jnp.sum(pair_q.astype(f32) * pair_h.astype(f32), axis=1)
    part_in = lax.dot_general(
        p_emb, panel_q, (((1,), (1,)), ((), ())), preferred_element_type=f32
    )
    part = jnp.concatenate([part_in, jnp.pad(part_pair.reshape(3, 128), ((0, 5), (0, 0)))], 1)
    score = (part + lax.ppermute(part, "mp", SWAP)) / normalizer_divisor
    s_in = score[:, :1024]
    s_pair = score[:3, 1024:].reshape(-1)
    e_in = jnp.exp(s_in)
    e_pair = jnp.where(valid, jnp.exp(s_pair), 0.0)
    eye = (
        lax.broadcasted_iota(jnp.int32, (8, 1024), 0)
        == lax.broadcasted_iota(jnp.int32, (8, 1024), 1)
    )
    spread = jnp.where(pick_q, e_pair[:, None], 0.0)
    z_part = jnp.sum(e_in, axis=0) + jnp.sum(spread, axis=0)
    w_part = jnp.sum(e_in * s_in, axis=0) + jnp.sum(spread * s_pair[:, None], axis=0)
    weights = jnp.concatenate([jnp.where(eye, 0.0, e_in), spread], 0).astype(bf16)
    sources = jnp.concatenate([p_emb, pair_h], 0)
    pulled = lax.dot_general(
        weights, sources, (((0,), (0,)), ((), ())), preferred_element_type=f32
    ).astype(bf16)
    for axis in ("c", "x", "z", "yh"):
        pulled = scatter_axis(pulled, axis)

    sums = sum_relative(jnp.concatenate([z_part.reshape(8, 128), w_part.reshape(8, 128)], 0))
    z_all = sums[:8].reshape(-1)
    c_in = (e_in / z_all[None, :] - eye.astype(f32)).astype(bf16)
    z_pair = jnp.sum(jnp.where(pick_q, z_all[None, :], 0.0), axis=1)
    c_pair = jnp.where(valid, e_pair / z_pair, 0.0).astype(bf16)
    ge_p = jnp.dot(c_in, panel_q, preferred_element_type=f32) / normalizer_divisor
    dot_p = jnp.sum(c_in.astype(f32) * s_in, axis=1)
    c_rows = jnp.where(pick_h, c_pair[:, None], jnp.zeros((), bf16))
    ge_h = (
        lax.dot_general(c_rows, pair_q, (((0,), (0,)), ((), ())), preferred_element_type=f32)
        / normalizer_divisor
    )
    dot_h = jnp.sum(c_rows.astype(f32) * s_pair[:, None], axis=0)
    z_own, w_own = sums[0, :8], sums[8, :8]
    s_own = jnp.sum(jnp.where(eye, s_in, 0.0), axis=1)
    e_own = jnp.exp(s_own)
    dot_q = w_own / z_own - s_own

    grad_p, direct_p = back(p_vals, gain, p_scale, p_length, ge_p, dot_p)
    grad_h, direct_h = back(h_vals, gain, h_scale, h_length, ge_h, dot_h)
    direct_q = q_vals * (q_scale / q_length)[:, None]
    gain_part = (
        jnp.sum(direct_p * (2.0 * ge_p - direct_p * gain * dot_p[:, None]), axis=0)
        + jnp.sum(direct_h * (2.0 * ge_h - direct_h * gain * dot_h[:, None]), axis=0)
        - jnp.sum(direct_q * direct_q * gain * dot_q[:, None], axis=0)
    )
    loss_part = jnp.sum(jnp.log(z_own) - s_own)
    packed = jnp.concatenate(
        [gain_part.reshape(16, 128), jnp.broadcast_to(loss_part, (8, 128))], 0
    )
    packed = sum_all(packed)

    ge_q = (
        pulled.astype(f32) / z_own[:, None]
        + (e_own / z_own - 1.0)[:, None] * p_emb.astype(f32)
    ) / normalizer_divisor
    grad_q, _ = back(q_vals, gain, q_scale, q_length, ge_q, dot_q)
    return grad_q, grad_p, grad_h, packed[:16].reshape(-1), packed[16, 0] / 1024


def solution(mesh):
    return jax.shard_map(
        local,
        mesh=mesh,
        in_specs=(
            P("dp", "mp"),
            P("dp", "mp"),
            P("dp", "mp"),
            P("mp"),
            P("dp", None, None),
            P("dp", None),
        ),
        out_specs=(P("dp", "mp"), P("dp", "mp"), P("dp", "mp"), P("mp"), P()),
        check_vma=False,
    )
```

```python
import functools

import jax
import jax.numpy as jnp
from jax import lax
from jax.experimental import pallas as pl
from jax.experimental.pallas import tpu as pltpu
from jax.sharding import PartitionSpec as P

D = 4096
normalizer_divisor = 0.02
eps_norm = 1e-06
f32 = jnp.float32
bf16 = jnp.bfloat16
C, X, Z, YH = 1, (2, 4), (8, 16, 32), 64
SWAP = [(0, 1), (1, 0)]


def flip(x, mask):
    return lax.ppermute(x, "dp", [(i, i ^ mask) for i in range(128)])


def double(x, mask):
    return jnp.concatenate([x, flip(x, mask)], 0)


STEPS = ((Z[0], 64), (Z[1], 32), (Z[2], 16), (YH, 8))


def stats(values, gain):
    squares = values * values
    return jnp.sum(squares, axis=1), jnp.sum(squares * gain * gain, axis=1)


def scales(total_sq, total_gsq):
    scale = lax.rsqrt(total_sq / D + eps_norm)
    length = jnp.sqrt(scale * scale * total_gsq + eps_norm)
    return scale, length


def back_rows(values, gain, scale, length, grad_unit, dot):
    ratio = (scale / length)[:, None]
    return (
        ratio * gain * (grad_unit - values * ratio * gain * dot[:, None])
        - values * (scale * scale * dot * eps_norm / (length * length * D))[:, None]
    ).astype(bf16)


def tie(*arrays):
    return lax.optimization_barrier(arrays)


def requests(hard_owner, hard_slot):
    owner = hard_owner.reshape(-1)
    slot = hard_slot.reshape(-1)
    number = jnp.arange(owner.shape[0], dtype=jnp.int32)
    earlier = (owner[:, None] == owner[None, :]) & (number[:, None] < number[None, :])
    position = jnp.sum(earlier.astype(jnp.int32), axis=0)
    low = slot % 256
    high = 1 + slot // 256 + 2 * (number // hard_slot.shape[1])
    place = jnp.arange(8, dtype=jnp.int32)[:, None]
    coded = jnp.where(
        place // 2 == position[None, :], jnp.where(place % 2 == 0, low[None, :], high[None, :]), 0
    ).astype(bf16)
    names = (owner[:, None] == jnp.arange(128, dtype=jnp.int32)[None, :]).astype(bf16)
    return jnp.dot(coded, names, preferred_element_type=f32).astype(bf16)


def diagonal(rows):
    shape = (rows, 128)
    return lax.broadcasted_iota(jnp.int32, shape, 0) == lax.broadcasted_iota(jnp.int32, shape, 1)


def as_row(column):
    return jnp.sum(jnp.where(diagonal(column.shape[0]), column, 0.0), axis=0, keepdims=True)


def as_column(row, rows):
    return jnp.sum(jnp.where(diagonal(rows), row, 0.0), axis=1, keepdims=True)


def score_kernel(panel, passages, gain, *refs):
    pair_q, near, out = refs[:4], refs[4:8], refs[8]
    g = gain[...]
    rows = panel[:, :2048]
    scaled = passages[...].astype(f32) * g
    high = scaled.astype(bf16)
    low = (scaled - high.astype(f32)).astype(bf16)
    contract = (((1,), (1,)), ((), ()))
    out[0:64] = lax.dot_general(
        high, rows, contract, preferred_element_type=f32
    ) + lax.dot_general(low, rows, contract, preferred_element_type=f32)
    values = rows.astype(f32)
    squares = values * values
    out[64:65] = as_row(jnp.sum(squares, axis=1, keepdims=True))
    out[65:66] = as_row(jnp.sum(squares * (g * g), axis=1, keepdims=True))
    for s in range(4):
        product = pair_q[s][...].astype(f32) * near[s][...].astype(f32) * g
        out[66 + s : 67 + s] = as_row(jnp.sum(product, axis=1, keepdims=True))
    out[70:72] = jnp.zeros((2, 128), f32)


def route_kernel(me_ref, asked, panel, table_a, table_b, *refs):
    near, pair_q, query, slots = refs[:4], refs[4:8], refs[8], refs[9]
    me = me_ref[0]
    row = lax.broadcasted_iota(jnp.int32, (96, 128), 0)
    entry = row >> 4
    entry = jnp.where(entry >= 3, 2 * entry - 5, 2 * entry)
    pick = (lax.broadcasted_iota(jnp.int32, (96, 128), 1) == (row & 15) * 8 + entry).astype(bf16)
    lane = lax.broadcasted_iota(jnp.int32, (96, 128), 1)
    block = lax.broadcasted_iota(jnp.int32, (48, 1), 0) & 15

    def decode(entries, column):
        values = jnp.sum(jnp.where(lane == column, entries, 0.0), axis=1, keepdims=True)
        low, high = values[:48].astype(jnp.int32), values[48:].astype(jnp.int32)
        slot = jnp.where(high > 0, low + 256 * ((high - 1) & 1), -1)
        return slot, jnp.where(high > 0, block * 8 + ((high - 1) >> 1), -1)

    def row_of(index):
        return as_row((index + 1).astype(f32)).astype(jnp.int32) - 1

    def one_hot(index, count):
        lanes = lax.broadcasted_iota(jnp.int32, (index.shape[0], count), 1)
        return (lanes == index).astype(f32)

    picks = ([], [])
    for s in range(4):
        entries = jnp.dot(pick, asked[s], preferred_element_type=f32)
        for t in range(2):
            slot, _ = decode(entries, me ^ t)
            picks[t].append(one_hot(slot, 512))
            slots[4 * t + s : 4 * t + s + 1] = row_of(slot)
        if s == 0:
            mine = entries
    rows = [
        jnp.dot(
            jnp.concatenate(picks[t], 0).astype(bf16), table[...], preferred_element_type=f32
        ).astype(bf16)
        for t, table in enumerate((table_a, table_b))
    ]
    for s in range(4):
        for t in range(2):
            near[s][48 * t : 48 * t + 48] = rows[t][48 * s : 48 * s + 48]
        index = jnp.concatenate([decode(mine, me ^ (2 * s + t))[1] for t in range(2)], 0)
        query[s : s + 1] = row_of(index)
        pair_q[s][...] = jnp.dot(
            one_hot(index, 128).astype(bf16), panel[:, :2048], preferred_element_type=f32
        ).astype(bf16)
    query[4:8] = jnp.full((4, 128), -1, jnp.int32)


def put_sums(message, rows, v):
    high = v.astype(bf16).astype(f32)
    middle = (v - high).astype(bf16).astype(f32)
    parts = [high, middle, v - high - middle, jnp.zeros((10, 128), f32)]
    message[rows : rows + 16, :128] = jnp.concatenate(parts, 0).astype(bf16)
    message[rows : rows + 16, 128:] = jnp.zeros((16, 1920), bf16)


def swap_lanes(v, bit):
    v = jnp.concatenate([v, jnp.zeros((6, 128), f32)], 0)
    lane = lax.broadcasted_iota(jnp.int32, (8, 128), 1)
    swapped = jnp.where(
        (lane & bit) > 0, pltpu.roll(v, bit, axis=1), pltpu.roll(v, 128 - bit, axis=1)
    )
    return swapped[:2]


def halve_kernel(bit, kept, got, sums, *refs):
    rows = kept.shape[0]
    total = kept[...].astype(f32) + got[:rows].astype(f32)
    if rows > 8:
        add = got[rows : rows + 16, :128].astype(f32)
        add = add[:2] + add[2:4] + add[4:6]
    else:
        add = got[8:10, :128]
    v = sums[0:2] + swap_lanes(add, bit)
    refs[0][0:2] = v
    refs[0][2:8] = jnp.zeros((6, 128), f32)
    half = rows // 2
    refs[1][...] = total[:half].astype(refs[1].dtype) if rows > 8 else total
    if rows > 16:
        refs[2][:half] = total[half:].astype(bf16)
        put_sums(refs[2], half, v)
    elif rows > 8:
        refs[2][0:8] = total[8:]
        refs[2][8:16, :128] = jnp.concatenate([v, jnp.zeros((6, 128), f32)], 0)
        refs[2][8:16, 128:] = jnp.zeros((8, 1920), f32)


def halve(kept, message, sums, mask, bit):
    rows = kept.shape[0]
    shapes = [jax.ShapeDtypeStruct((8, 128), f32)]
    if rows > 16:
        shapes.append(jax.ShapeDtypeStruct((rows // 2, 2048), bf16))
        shapes.append(jax.ShapeDtypeStruct((rows // 2 + 16, 2048), bf16))
    elif rows > 8:
        shapes.append(jax.ShapeDtypeStruct((8, 2048), f32))
        shapes.append(jax.ShapeDtypeStruct((16, 2048), f32))
    else:
        shapes.append(jax.ShapeDtypeStruct((8, 2048), f32))
    sums, kept, *message = call(functools.partial(halve_kernel, bit), *shapes)(
        kept, flip(message, mask), sums
    )
    return kept, message[0] if message else None, sums


def pull_kernel(part, got, query, passages, *refs):
    near, kept, message, sums, small = refs[:4], refs[4], refs[5], refs[6], refs[7]
    full = part[...] + got[...]
    scale = lax.rsqrt(full[64:65] / D + eps_norm)
    length = jnp.sqrt(scale * scale * full[65:66] + eps_norm)
    ratio = scale / length
    ratio_column = as_column(ratio, 128)
    s_in = full[:64] * ratio / normalizer_divisor
    e_in = jnp.exp(s_in)
    own = diagonal(64) & (lax.broadcasted_iota(jnp.int32, (64, 128), 0) < 8)
    total = lax.dot_general(
        jnp.where(own, 0.0, e_in).astype(bf16),
        passages[...],
        (((0,), (0,)), ((), ())),
        preferred_element_type=f32,
    )
    z = jnp.zeros((128, 1), f32)
    w = jnp.zeros((128, 1), f32)
    for s in range(4):
        asker = query[s : s + 1, :]
        pick = lax.broadcasted_iota(jnp.int32, (128, 128), 0) == asker
        ratio_pair = jnp.sum(jnp.where(pick, ratio_column, 0.0), axis=0, keepdims=True)
        s_pair = full[66 + s : 67 + s] * ratio_pair / normalizer_divisor
        e_pair = jnp.where(asker >= 0, jnp.exp(s_pair), 0.0)
        spread = jnp.where(pick, e_pair, 0.0)
        z = z + jnp.sum(spread, axis=1, keepdims=True)
        w = w + jnp.sum(spread * s_pair, axis=1, keepdims=True)
        total = total + jnp.dot(
            spread[:, :96].astype(bf16), near[s][...], preferred_element_type=f32
        )
        small[66 + s : 67 + s] = s_pair
        small[70 + s : 71 + s] = e_pair
        small[74 + s : 75 + s] = ratio_pair
    kept[...] = total[:64].astype(bf16)
    message[0:64] = total[64:].astype(bf16)
    small[0:64] = s_in
    z = jnp.sum(e_in, axis=0, keepdims=True) + as_row(z)
    w = jnp.sum(e_in * s_in, axis=0, keepdims=True) + as_row(w)
    v = jnp.concatenate([z, w], 0)
    put_sums(message, 64, v)
    sums[0:2] = v
    sums[2:8] = jnp.zeros((6, 128), f32)
    small[64:66] = v
    small[78:79] = scale
    small[79:80] = length


def weigh_kernel(sums, small, query, panel, passages, gain, own_ref, *refs):
    pair_q, near, packed, late = refs[:4], refs[4:8], refs[8], refs[9:13]
    g = gain[...]
    z, w = sums[0:1], sums[1:2]
    s_in = small[0:64]
    scale, length = small[78:79], small[79:80]
    ratio = scale / length
    own = diagonal(64) & (lax.broadcasted_iota(jnp.int32, (64, 128), 0) < 8)
    c_in = ((jnp.exp(s_in) / z - jnp.where(own, 1.0, 0.0)) * ratio).astype(bf16)
    grads = jnp.dot(c_in, panel[:, :2048], preferred_element_type=f32)
    dots = jnp.sum(c_in.astype(f32) * (s_in / ratio), axis=1, keepdims=True)
    z_column = as_column(z, 128)
    values = passages[...].astype(f32)
    first = jnp.sum(grads * values, axis=0, keepdims=True)
    second = jnp.sum(values * values * dots, axis=0, keepdims=True)
    for s in range(4):
        asker = query[s : s + 1, :]
        pick = lax.broadcasted_iota(jnp.int32, (128, 128), 0) == asker
        z_pair = jnp.sum(jnp.where(pick, z_column, 0.0), axis=0, keepdims=True)
        c_pair = jnp.where(asker >= 0, small[70 + s : 71 + s] / z_pair, 0.0)
        ratio_pair = small[74 + s : 75 + s]
        coeff = (c_pair * ratio_pair).astype(bf16).astype(f32)
        pair_dot = jnp.where(asker >= 0, coeff * small[66 + s : 67 + s] / ratio_pair, 0.0)
        h = near[s][...].astype(f32)
        first = first + jnp.sum(
            pair_q[s][...].astype(f32) * h * as_column(coeff, 96), axis=0, keepdims=True
        )
        second = second + jnp.sum(h * h * as_column(pair_dot, 96), axis=0, keepdims=True)
        late[s][0:8, :2048] = grads[8 * s : 8 * s + 8]
        late[s][8:16, :2048] = grads[8 * s + 32 : 8 * s + 40]
        late[s][0:1, 2048:] = coeff
        late[s][1:2, 2048:] = pair_dot
        late[s][2:3, 2048:] = as_row(
            jnp.concatenate([dots[8 * s : 8 * s + 8], dots[8 * s + 32 : 8 * s + 40]], 0)
        )
        late[s][3:16, 2048:] = jnp.zeros((13, 128), f32)
    s_own = jnp.sum(jnp.where(own, s_in, 0.0), axis=0, keepdims=True)
    dot_own = as_column(w / z - s_own, 8)
    ratio_own = as_column(ratio, 8)
    direct = own_ref[...].astype(f32) * ratio_own
    third = jnp.sum(direct * direct * g * dot_own, axis=0, keepdims=True)
    result = first * (2.0 / normalizer_divisor) - second / g - third
    for i in range(16):
        packed[i : i + 1] = result[:, 128 * i : 128 * i + 128]
    lane = lax.broadcasted_iota(jnp.int32, (1, 128), 1)
    loss = jnp.sum(jnp.where(lane < 8, jnp.log(z) - s_own, 0.0), axis=1, keepdims=True)
    packed[16:24] = jnp.broadcast_to(loss, (8, 128))


def call(kernel, *shapes):
    return pl.pallas_call(
        kernel,
        out_shape=shapes,
        compiler_params=pltpu.CompilerParams(vmem_limit_bytes=40 * 1024 * 1024),
    )


def local(query_hidden, passage_hidden, hard_hidden, gain, hard_owner, hard_slot):
    me = lax.axis_index("dp")
    p_vals = passage_hidden.astype(f32)
    h_vals = hard_hidden.astype(f32)
    p_sq, p_gsq = stats(p_vals, gain)
    h_sq, h_gsq = stats(h_vals, gain)
    mine = jnp.concatenate([p_sq, p_gsq, h_sq, h_gsq])
    table = requests(hard_owner, hard_slot)
    panel = double(jnp.concatenate([query_hidden, table], 1), YH)
    panel, mine = tie(panel, mine)
    panel = double(panel, Z[2])
    tot = mine + lax.ppermute(mine, "mp", SWAP)
    panel, tot = tie(panel, tot)
    panel = double(panel, Z[1])
    p_scale, p_length = scales(tot[:8], tot[8:16])
    h_scale, h_length = scales(tot[16:528], tot[528:])
    p_emb = (p_vals * (p_scale / p_length)[:, None] * gain).astype(bf16)
    h_emb = (h_vals * (h_scale / h_length)[:, None] * gain).astype(bf16)
    panel, p_emb, h_emb = tie(panel, p_emb, h_emb)
    panel = double(panel, Z[0])
    p_all = jnp.concatenate([p_emb] + [flip(p_emb, 2 * s) for s in (1, 2, 3)], 0)
    h_other = flip(h_emb, C)
    panel, p_all, h_other = tie(panel, p_all, h_other)
    asked = panel[:, 2048:]
    asked = jnp.stack([asked] + [flip(asked, 2 * s) for s in (1, 2, 3)])
    p_all = jnp.concatenate([p_all, flip(p_all, C)], 0)

    wide = jax.ShapeDtypeStruct((96, 2048), bf16)
    index = jax.ShapeDtypeStruct((8, 128), jnp.int32)
    *both, query, slots = pl.pallas_call(
        route_kernel,
        out_shape=[wide] * 8 + [index] * 2,
        in_specs=[pl.BlockSpec(memory_space=pltpu.SMEM)] + [pl.BlockSpec(memory_space=pltpu.VMEM)] * 4,
        compiler_params=pltpu.CompilerParams(vmem_limit_bytes=40 * 1024 * 1024),
    )(me[None], asked, panel, h_emb, h_other)
    near, pair_q = both[:4], both[4:]
    near = [near[0]] + [flip(near[s], 2 * s) for s in (1, 2, 3)]
    gain_row = gain[None]

    (part,) = call(score_kernel, jax.ShapeDtypeStruct((72, 128), f32))(
        panel, p_all, gain_row, *pair_q, *near
    )
    got = lax.ppermute(part, "mp", SWAP)
    kept, message, sums, small = call(
        pull_kernel,
        jax.ShapeDtypeStruct((64, 2048), bf16),
        jax.ShapeDtypeStruct((80, 2048), bf16),
        jax.ShapeDtypeStruct((8, 128), f32),
        jax.ShapeDtypeStruct((80, 128), f32),
    )(part, got, query, p_all, *near)
    back = [pair_q[0]] + [flip(pair_q[s], 2 * s) for s in (1, 2, 3)]
    for mask, bit in STEPS:
        kept, message, sums = halve(kept, message, sums, mask, bit)
    pulled, sums, *back = tie(kept, sums, *back)
    packed, *late = call(
        weigh_kernel,
        jax.ShapeDtypeStruct((24, 128), f32),
        *[jax.ShapeDtypeStruct((16, 2176), f32)] * 4,
    )(sums, small, query, panel, p_all, gain_row, query_hidden, *pair_q, *near)
    packed = packed + flip(packed, C)
    packed, *late = tie(packed, *late)
    pair_q_other = flip(jnp.concatenate([block[48:] for block in back], 0), C)
    slot_other = flip(slots[4:], C)
    z_own, w_own = sums[0, :8], sums[1, :8]
    s_own = jnp.sum(jnp.where(jnp.eye(8, dtype=bool), small[:8, :8], 0.0), axis=1)
    e_own = jnp.exp(s_own)
    dot_q = w_own / z_own - s_own
    q_vals = query_hidden.astype(f32)
    q_scale, q_length = small[78, :8], small[79, :8]
    late = [late[0]] + [flip(late[s], 2 * s) for s in (1, 2, 3)]
    for mask in X:
        packed = packed + flip(packed, mask)
    packed, *late = tie(packed, *late)

    ge_p = sum(block[:, :2048] for block in late)
    dot_p = sum(block[2, 2048:2064] for block in late)
    coeff = jnp.concatenate([block[0, 2048:2144] for block in late]).reshape(4, 2, 48)
    pair_dot = jnp.concatenate([block[1, 2048:2144] for block in late]).reshape(4, 2, 48)
    give = jnp.concatenate(
        [
            ge_p[8:],
            jnp.concatenate(
                [
                    jnp.pad(coeff[:, 1].reshape(1, 192), ((0, 0), (0, 64))),
                    jnp.pad(pair_dot[:, 1].reshape(1, 192), ((0, 0), (0, 64))),
                    jnp.pad(dot_p[None, 8:], ((0, 0), (0, 248))),
                    jnp.zeros((5, 256), f32),
                ],
                0,
            ),
        ],
        1,
    )
    got = flip(give, C)
    packed = packed + flip(packed, Z[0])
    packed, got = tie(packed, got)
    for mask in (Z[1], Z[2], YH):
        packed = packed + flip(packed, mask)
    ge_p = (ge_p[:8] + got[:, :2048]) * gain / normalizer_divisor
    dot_p = dot_p[:8] + got[2, 2048:2056]
    coeff = jnp.concatenate([coeff[:, 0].reshape(-1), got[0, 2048:2240]])
    pair_dot = jnp.concatenate([pair_dot[:, 0].reshape(-1), got[1, 2048:2240]])
    slot = jnp.concatenate([slots[:4, :48].reshape(-1), slot_other[:, :48].reshape(-1)])
    pick_h = slot[:, None] == jnp.arange(512, dtype=jnp.int32)[None, :]
    ge_h = (
        lax.dot_general(
            jnp.where(pick_h, coeff[:, None], 0.0).astype(bf16),
            jnp.concatenate([block[:48] for block in back] + [pair_q_other], 0),
            (((0,), (0,)), ((), ())),
            preferred_element_type=f32,
        )
        * gain
        / normalizer_divisor
    )
    dot_h = jnp.sum(jnp.where(pick_h, pair_dot[:, None], 0.0), axis=0)
    grad_p = back_rows(p_vals, gain, p_scale, p_length, ge_p, dot_p)
    grad_h = back_rows(h_vals, gain, h_scale, h_length, ge_h, dot_h)
    ge_q = (
        pulled / z_own[:, None]
        + (e_own / z_own - 1.0)[:, None] * p_emb.astype(f32)
    ) / normalizer_divisor
    grad_q = back_rows(q_vals, gain, q_scale, q_length, ge_q, dot_q)
    return grad_q, grad_p, grad_h, packed[:16].reshape(-1), packed[16, 0] / 1024


def solution(mesh):
    return jax.shard_map(
        local,
        mesh=mesh,
        in_specs=(
            P("dp", "mp"),
            P("dp", "mp"),
            P("dp", "mp"),
            P("mp"),
            P("dp", None, None),
            P("dp", None),
        ),
        out_specs=(P("dp", "mp"), P("dp", "mp"), P("dp", "mp"), P("mp"), P()),
        check_vma=False,
    )
```

```python
import functools

import jax
import jax.numpy as jnp
from jax import lax
from jax.experimental import pallas as pl
from jax.experimental.pallas import tpu as pltpu
from jax.sharding import PartitionSpec as P

D = 4096
normalizer_divisor = 0.02
eps_norm = 1e-06
f32 = jnp.float32
bf16 = jnp.bfloat16
C, X, Z, YH = 1, (2, 4), (8, 16, 32), 64
SWAP = [(0, 1), (1, 0)]


def flip(x, mask):
    return lax.ppermute(x, "dp", [(i, i ^ mask) for i in range(128)])


def double(x, mask):
    return jnp.concatenate([x, flip(x, mask)], 0)


def stats(values, gain):
    squares = values * values
    return jnp.sum(squares, axis=1), jnp.sum(squares * gain * gain, axis=1)


def scales(total_sq, total_gsq):
    scale = lax.rsqrt(total_sq / D + eps_norm)
    length = jnp.sqrt(scale * scale * total_gsq + eps_norm)
    return scale, length


def tie(*arrays):
    return lax.optimization_barrier(arrays)


def requests(hard_owner, hard_slot):
    owner = hard_owner.reshape(-1)
    slot = hard_slot.reshape(-1)
    number = jnp.arange(owner.shape[0], dtype=jnp.int32)
    earlier = (owner[:, None] == owner[None, :]) & (number[:, None] < number[None, :])
    position = jnp.sum(earlier.astype(jnp.int32), axis=0)
    low = slot % 256
    high = 1 + slot // 256 + 2 * (number // hard_slot.shape[1])
    place = jnp.arange(8, dtype=jnp.int32)[:, None]
    coded = jnp.where(
        place // 2 == position[None, :], jnp.where(place % 2 == 0, low[None, :], high[None, :]), 0
    ).astype(bf16)
    names = (owner[:, None] == jnp.arange(128, dtype=jnp.int32)[None, :]).astype(bf16)
    return jnp.dot(coded, names, preferred_element_type=f32).astype(bf16)


def diagonal(rows):
    shape = (rows, 128)
    return lax.broadcasted_iota(jnp.int32, shape, 0) == lax.broadcasted_iota(jnp.int32, shape, 1)


def as_row(column):
    return jnp.sum(jnp.where(diagonal(column.shape[0]), column, 0.0), axis=0, keepdims=True)


def as_column(row, rows):
    return jnp.sum(jnp.where(diagonal(rows), row, 0.0), axis=1, keepdims=True)


def score_kernel(panel, passages, gain, *refs):
    pair_q, near, out = refs[:4], refs[4:8], refs[8]
    g = gain[...]
    rows = panel[:, :2048]
    scaled = passages[...].astype(f32) * g
    high = scaled.astype(bf16)
    low = (scaled - high.astype(f32)).astype(bf16)
    contract = (((1,), (1,)), ((), ()))
    out[0:64] = lax.dot_general(
        high, rows, contract, preferred_element_type=f32
    ) + lax.dot_general(low, rows, contract, preferred_element_type=f32)
    values = rows.astype(f32)
    squares = values * values
    out[64:65] = as_row(jnp.sum(squares, axis=1, keepdims=True))
    out[65:66] = as_row(jnp.sum(squares * (g * g), axis=1, keepdims=True))
    for s in range(4):
        product = pair_q[s][...].astype(f32) * near[s][...].astype(f32) * g
        out[66 + s : 67 + s] = as_row(jnp.sum(product, axis=1, keepdims=True))
    out[70:72] = jnp.zeros((2, 128), f32)


def entry_columns(asked):
    row = lax.broadcasted_iota(jnp.int32, (96, 128), 0)
    entry = row >> 4
    entry = jnp.where(entry >= 3, 2 * entry - 5, 2 * entry)
    pick = (lax.broadcasted_iota(jnp.int32, (96, 128), 1) == (row & 15) * 8 + entry).astype(bf16)
    return jnp.dot(pick, asked, preferred_element_type=f32)


def decode(entries, column):
    lane = lax.broadcasted_iota(jnp.int32, (96, 128), 1)
    block = lax.broadcasted_iota(jnp.int32, (48, 1), 0) & 15
    values = jnp.sum(jnp.where(lane == column, entries, 0.0), axis=1, keepdims=True)
    low, high = values[:48].astype(jnp.int32), values[48:].astype(jnp.int32)
    slot = jnp.where(high > 0, low + 256 * ((high - 1) & 1), -1)
    return slot, jnp.where(high > 0, block * 8 + ((high - 1) >> 1), -1)


def row_of(index):
    return as_row((index + 1).astype(f32)).astype(jnp.int32) - 1


def one_hot(index, count):
    lanes = lax.broadcasted_iota(jnp.int32, (index.shape[0], count), 1)
    return (lanes == index).astype(f32)


def asker_kernel(me_ref, panel, *refs):
    pair_q, query = refs[:4], refs[4]
    me = me_ref[0]
    entries = entry_columns(panel[:, 2048:])
    for s in range(4):
        index = jnp.concatenate([decode(entries, me ^ (2 * s + t))[1] for t in range(2)], 0)
        query[s : s + 1] = row_of(index)
        pair_q[s][...] = jnp.dot(
            one_hot(index, 128).astype(bf16), panel[:, :2048], preferred_element_type=f32
        ).astype(bf16)
    query[4:8] = jnp.full((4, 128), -1, jnp.int32)


def owner_kernel(me_ref, panel, table_a, table_b, ratios, gain, *refs):
    asked, near, slots = refs[:3], refs[3:7], refs[7]
    me = me_ref[0]
    picks = ([], [])
    for s in range(4):
        entries = entry_columns(panel[:, 2048:] if s == 0 else asked[s - 1][...])
        both = [decode(entries, me ^ t)[0] for t in range(2)]
        for t in range(2):
            picks[t].append(one_hot(both[t], 512))
        slots[s : s + 1] = row_of(jnp.concatenate(both, 0))
    slots[4:8] = jnp.full((4, 128), -1, jnp.int32)
    for t, table in enumerate((table_a, table_b)):
        pick_h = jnp.concatenate(picks[t], 0)
        ratio = jnp.sum(jnp.where(pick_h > 0, ratios[t : t + 1], 0.0), axis=1, keepdims=True)
        values = jnp.dot(pick_h.astype(bf16), table[...], preferred_element_type=f32)
        values = (values * ratio * gain[...]).astype(bf16)
        for s in range(4):
            near[s][48 * t : 48 * t + 48] = values[48 * s : 48 * s + 48]


def split_sums(v):
    high = v.astype(bf16).astype(f32)
    middle = (v - high).astype(bf16).astype(f32)
    parts = [high, middle, v - high - middle, jnp.zeros((10, 128), f32)]
    return jnp.concatenate(parts, 0).astype(bf16)


def swap_lanes(v, bits):
    lane = lax.broadcasted_iota(jnp.int32, (8, 128), 1)
    for bit in (8, 16, 32, 64):
        if bits & bit:
            v = jnp.where(
                (lane & bit) > 0, pltpu.roll(v, bit, axis=1), pltpu.roll(v, 128 - bit, axis=1)
            )
    return v


def add_kernel(kept, sums, *refs):
    got, out, message, out_sums = refs[:7], refs[7], refs[8], refs[9]
    total = kept[...]
    v = sums[...]
    zeros = jnp.zeros((6, 128), f32)
    for m in range(1, 8):
        block = got[m - 1][...].astype(f32)
        total = total + block[:, :2048]
        extra = block[:, 2048:]
        extra = jnp.concatenate([extra[0:2] + extra[2:4] + extra[4:6], zeros], 0)
        v = v + swap_lanes(extra, 16 * m)
    out[...] = total[:8]
    message[0:8] = total[8:]
    message[8:16, :128] = v
    message[8:16, 128:] = jnp.zeros((8, 1920), f32)
    out_sums[...] = v


def late_kernel(slots, *refs):
    arrived, own, give, late, done = refs[:4], refs[4], refs[5], refs[6], refs[7]
    copies = [pltpu.make_async_copy(arrived[s], late.at[s], done.at[s]) for s in range(4)]
    for copy in copies:
        copy.start()
    for copy in copies:
        copy.wait()
    own[...] = sum(late[s, 0:8, :2048] for s in range(4))
    give[0:8, :2048] = sum(late[s, 8:16, :2048] for s in range(4))
    give[8:16, :2048] = jnp.zeros((8, 2048), f32)
    for s in range(4):
        give[s : s + 1, 2048:] = late[s, 0:1, 2048:]
        give[4 + s : 5 + s, 2048:] = late[s, 1:2, 2048:]
    give[8:9, 2048:] = sum(late[s, 2:3, 2048:] for s in range(4))
    give[9:13, 2048:] = slots[0:4].astype(f32)
    give[13:16, 2048:] = jnp.zeros((3, 128), f32)


def pack_kernel(*refs):
    back, other, rows, done = refs[:4], refs[4], refs[5], refs[6]
    copies = [
        pltpu.make_async_copy(back[s].at[48:96], rows.at[48 * s : 48 * s + 48], done.at[s])
        for s in range(4)
    ]
    for copy in copies:
        copy.start()
    for copy in copies:
        copy.wait()
    other[...] = rows[...]


def finish(values, ratio, tail, g, grad, dot):
    return (ratio * g * (grad - values * ratio * g * dot) - values * (tail * dot)).astype(bf16)


def hard_kernel(hidden_ref, passages, gain, totals, own_ref, give_ref, got_ref, *refs):
    back, other, out, out_p = refs[:4], refs[4], refs[5], refs[6]
    rows, hidden, own, give, got, done = refs[7:]
    copies = [
        pltpu.make_async_copy(own_ref, own, done.at[8]),
        pltpu.make_async_copy(give_ref, give, done.at[9]),
        pltpu.make_async_copy(got_ref, got, done.at[10]),
    ]
    for s in range(4):
        first, second = rows.at[128 * s : 128 * s + 48], rows.at[128 * s + 48 : 128 * s + 96]
        copies.append(pltpu.make_async_copy(back[s].at[0:48], first, done.at[2 * s]))
        copies.append(
            pltpu.make_async_copy(other.at[48 * s : 48 * s + 48], second, done.at[2 * s + 1])
        )
    pieces = [
        pltpu.make_async_copy(
            hidden_ref.at[128 * i : 128 * i + 128],
            hidden.at[128 * i : 128 * i + 128],
            done.at[11 + i],
        )
        for i in range(4)
    ]
    for copy in copies + pieces:
        copy.start()
    for s in range(4):
        rows[128 * s + 96 : 128 * s + 128] = jnp.zeros((32, 2048), bf16)
    for copy in copies:
        copy.wait()
    g = gain[...]
    inverse = g / normalizer_divisor
    lane = lax.broadcasted_iota(jnp.int32, (16, 128), 1)
    facts = jnp.where(lane < 48, give[:, 2048:], got[:, 2048:])
    scale = lax.rsqrt(totals[0:1] / D + eps_norm)
    length = jnp.sqrt(scale * scale * totals[1:2] + eps_norm)
    ratio = scale / length
    tail = scale * scale * eps_norm / (length * length * D)
    slot = jnp.concatenate([facts[9 + s : 10 + s] for s in range(4)], 1).astype(jnp.int32)
    coeff = jnp.concatenate([facts[s : s + 1] for s in range(4)], 1)
    pair_dot = jnp.concatenate([facts[4 + s : 5 + s] for s in range(4)], 1)
    used = (lax.broadcasted_iota(jnp.int32, (1, 512), 1) & 127) < 96
    slot = jnp.where(used, slot, -1)
    for i in range(4):
        pick = lax.broadcasted_iota(jnp.int32, (128, 512), 0) + 128 * i == slot
        weights = jnp.where(pick, coeff, 0.0).astype(bf16)
        grad = jnp.dot(weights, rows[...], preferred_element_type=f32)
        dot = jnp.sum(jnp.where(pick, pair_dot, 0.0), axis=1, keepdims=True)
        part = slice(128 * i, 128 * i + 128)
        pieces[i].wait()
        values = hidden[part, :].astype(f32)
        ratio_part, tail_part = as_column(ratio[:, part], 128), as_column(tail[:, part], 128)
        out[part, :] = finish(values, ratio_part, tail_part, g, grad * inverse, dot)
    row = give[8:16, 2048:] + pltpu.roll(got[8:16, 2048:], 120, axis=1)
    dot = as_column(row[0:1], 8)
    grad = (own[...] + got[0:8, :2048]) * inverse
    out_p[...] = finish(
        passages[...].astype(f32),
        as_column(ratio[:, 512:640], 8),
        as_column(tail[:, 512:640], 8),
        g,
        grad,
        dot,
    )


def pull_kernel(part, got, query, passages, *refs):
    near, kept, messages, sums, small = refs[:4], refs[4], refs[5:12], refs[12], refs[13]
    full = part[...] + got[...]
    scale = lax.rsqrt(full[64:65] / D + eps_norm)
    length = jnp.sqrt(scale * scale * full[65:66] + eps_norm)
    ratio = scale / length
    ratio_column = as_column(ratio, 128)
    s_in = full[:64] * ratio / normalizer_divisor
    e_in = jnp.exp(s_in)
    own = diagonal(64) & (lax.broadcasted_iota(jnp.int32, (64, 128), 0) < 8)
    total = lax.dot_general(
        jnp.where(own, 0.0, e_in).astype(bf16),
        passages[...],
        (((0,), (0,)), ((), ())),
        preferred_element_type=f32,
    )
    z = jnp.zeros((128, 1), f32)
    w = jnp.zeros((128, 1), f32)
    for s in range(4):
        asker = query[s : s + 1, :]
        pick = lax.broadcasted_iota(jnp.int32, (128, 128), 0) == asker
        ratio_pair = jnp.sum(jnp.where(pick, ratio_column, 0.0), axis=0, keepdims=True)
        s_pair = full[66 + s : 67 + s] * ratio_pair / normalizer_divisor
        e_pair = jnp.where(asker >= 0, jnp.exp(s_pair), 0.0)
        spread = jnp.where(pick, e_pair, 0.0)
        z = z + jnp.sum(spread, axis=1, keepdims=True)
        w = w + jnp.sum(spread * s_pair, axis=1, keepdims=True)
        total = total + jnp.dot(
            spread[:, :96].astype(bf16), near[s][...], preferred_element_type=f32
        )
        small[66 + s : 67 + s] = s_pair
        small[70 + s : 71 + s] = e_pair
        small[74 + s : 75 + s] = ratio_pair
    kept[...] = total[:16]
    small[0:64] = s_in
    z = jnp.sum(e_in, axis=0, keepdims=True) + as_row(z)
    w = jnp.sum(e_in * s_in, axis=0, keepdims=True) + as_row(w)
    v = jnp.concatenate([z, w], 0)
    extra = split_sums(v)
    for m in range(1, 8):
        messages[m - 1][:, :2048] = total[16 * m : 16 * m + 16].astype(bf16)
        messages[m - 1][:, 2048:] = extra
    sums[0:2] = v
    sums[2:8] = jnp.zeros((6, 128), f32)
    small[64:66] = v
    small[78:79] = scale
    small[79:80] = length


def weigh_kernel(kept, got, sums, small, query, panel, passages, gain, own_ref, *refs):
    pair_q, near, packed, late, out_q = refs[:4], refs[4:8], refs[8], refs[9:13], refs[13]
    g = gain[...]
    pulled = kept[...] + got[0:8]
    total = sums[...] + swap_lanes(got[8:16, :128], 8)
    z, w = total[0:1], total[1:2]
    s_in = small[0:64]
    scale, length = small[78:79], small[79:80]
    ratio = scale / length
    own = diagonal(64) & (lax.broadcasted_iota(jnp.int32, (64, 128), 0) < 8)
    c_in = ((jnp.exp(s_in) / z - jnp.where(own, 1.0, 0.0)) * ratio).astype(bf16)
    grads = jnp.dot(c_in, panel[:, :2048], preferred_element_type=f32)
    dots = jnp.sum(c_in.astype(f32) * (s_in / ratio), axis=1, keepdims=True)
    z_column = as_column(z, 128)
    values = passages[...].astype(f32)
    first = jnp.sum(grads * values, axis=0, keepdims=True)
    second = jnp.sum(values * values * dots, axis=0, keepdims=True)
    for s in range(4):
        asker = query[s : s + 1, :]
        pick = lax.broadcasted_iota(jnp.int32, (128, 128), 0) == asker
        z_pair = jnp.sum(jnp.where(pick, z_column, 0.0), axis=0, keepdims=True)
        c_pair = jnp.where(asker >= 0, small[70 + s : 71 + s] / z_pair, 0.0)
        ratio_pair = small[74 + s : 75 + s]
        coeff = (c_pair * ratio_pair).astype(bf16).astype(f32)
        pair_dot = jnp.where(asker >= 0, coeff * small[66 + s : 67 + s] / ratio_pair, 0.0)
        h = near[s][...].astype(f32)
        first = first + jnp.sum(
            pair_q[s][...].astype(f32) * h * as_column(coeff, 96), axis=0, keepdims=True
        )
        second = second + jnp.sum(h * h * as_column(pair_dot, 96), axis=0, keepdims=True)
        late[s][0:8, :2048] = grads[8 * s : 8 * s + 8]
        late[s][8:16, :2048] = grads[8 * s + 32 : 8 * s + 40]
        late[s][0:1, 2048:] = coeff
        late[s][1:2, 2048:] = pair_dot
        late[s][2:3, 2048:] = as_row(
            jnp.concatenate([dots[8 * s : 8 * s + 8], dots[8 * s + 32 : 8 * s + 40]], 0)
        )
        late[s][3:16, 2048:] = jnp.zeros((13, 128), f32)
    s_own = jnp.sum(jnp.where(own, s_in, 0.0), axis=0, keepdims=True)
    dot_own = as_column(w / z - s_own, 8)
    ratio_own = as_column(ratio, 8)
    values = own_ref[...].astype(f32)
    direct = values * ratio_own
    z_own = as_column(z, 8)
    excess = jnp.exp(as_column(s_own, 8)) / z_own - 1.0
    grad = (pulled / z_own + excess * passages[0:8].astype(f32)) / normalizer_divisor
    own_scale, own_length = as_column(scale, 8), as_column(length, 8)
    tail = own_scale * own_scale * eps_norm / (own_length * own_length * D)
    out_q[...] = finish(values, ratio_own, tail, g, grad, dot_own)
    third = jnp.sum(direct * direct * g * dot_own, axis=0, keepdims=True)
    result = first * (2.0 / normalizer_divisor) - second / g - third
    for i in range(16):
        packed[i : i + 1] = result[:, 128 * i : 128 * i + 128]
    lane = lax.broadcasted_iota(jnp.int32, (1, 128), 1)
    loss = jnp.sum(jnp.where(lane < 8, jnp.log(z) - s_own, 0.0), axis=1, keepdims=True)
    packed[16:24] = jnp.broadcast_to(loss, (8, 128))


def call(kernel, *shapes, scratch=(), limit=14, fetched=(), scalar=False):
    def run(*operands):
        spaces = [pltpu.HBM if own else pltpu.VMEM for own in fetched]
        spaces = spaces or [pltpu.SMEM if scalar and not i else pltpu.VMEM for i in range(len(operands))]
        return pl.pallas_call(
            kernel,
            out_shape=shapes,
            in_specs=[pl.BlockSpec(memory_space=space) for space in spaces],
            scratch_shapes=scratch,
            compiler_params=pltpu.CompilerParams(vmem_limit_bytes=limit * 1024 * 1024),
        )(*operands)

    return run


def local(query_hidden, passage_hidden, hard_hidden, gain, hard_owner, hard_slot):
    me = lax.axis_index("dp")
    p_vals = passage_hidden.astype(f32)
    h_vals = hard_hidden.astype(f32)
    p_sq, p_gsq = stats(p_vals, gain)
    h_sq, h_gsq = stats(h_vals, gain)
    mine = jnp.stack([jnp.concatenate([h_sq, p_sq]), jnp.concatenate([h_gsq, p_gsq])])
    mine = jnp.pad(mine, ((0, 0), (0, 120)))
    table = requests(hard_owner, hard_slot)
    panel = double(jnp.concatenate([query_hidden, table], 1), YH)
    panel, mine = tie(panel, mine)
    panel = double(panel, Z[2])
    tot = mine + lax.ppermute(mine, "mp", SWAP)
    panel, tot = tie(panel, tot)
    panel = double(panel, Z[1])
    scale, length = scales(tot[0], tot[1])
    p_scale, p_length = scale[512:520], length[512:520]
    h_scale, h_length = scale[:512], length[:512]
    p_emb = (p_vals * (p_scale / p_length)[:, None] * gain).astype(bf16)
    ratios = (h_scale / h_length)[None]
    panel, p_emb, hard_other = tie(panel, p_emb, flip(hard_hidden, C))
    panel = double(panel, Z[0])
    p_all = jnp.concatenate([p_emb] + [flip(p_emb, 2 * s) for s in (1, 2, 3)], 0)
    ratios = jnp.concatenate([ratios, flip(ratios, C)], 0)
    panel, p_all = tie(panel, p_all)
    wide = jax.ShapeDtypeStruct((96, 2048), bf16)
    index = jax.ShapeDtypeStruct((8, 128), jnp.int32)
    *pair_q, query = call(asker_kernel, *[wide] * 4, index, scalar=True)(me[None], panel)
    asked = panel[:, 2048:]
    asked = [flip(asked, 2 * s) for s in (1, 2, 3)]
    p_all = jnp.concatenate([p_all, flip(p_all, C)], 0)
    *near, slots = call(owner_kernel, *[wide] * 4, index, scalar=True, limit=20)(
        me[None], panel, hard_hidden, hard_other, ratios, gain[None], *asked
    )
    near = [near[0]] + [flip(near[s], 2 * s) for s in (1, 2, 3)]
    gain_row = gain[None]

    (part,) = call(score_kernel, jax.ShapeDtypeStruct((72, 128), f32))(
        panel, p_all, gain_row, *pair_q, *near
    )
    got = lax.ppermute(part, "mp", SWAP)
    kept, *messages, sums, small = call(
        pull_kernel,
        jax.ShapeDtypeStruct((16, 2048), f32),
        *[jax.ShapeDtypeStruct((16, 2176), bf16)] * 7,
        jax.ShapeDtypeStruct((8, 128), f32),
        jax.ShapeDtypeStruct((80, 128), f32),
    )(part, got, query, p_all, *near)
    messages = [flip(message, mask) for message, mask in zip(messages, (32, 16, 48, 8, 40, 24, 56))]
    kept, message, sums = call(
        add_kernel,
        jax.ShapeDtypeStruct((8, 2048), f32),
        jax.ShapeDtypeStruct((16, 2048), f32),
        jax.ShapeDtypeStruct((8, 128), f32),
    )(kept, sums, *messages)
    kept, message, sums, first, third = tie(kept, message, sums, pair_q[1], pair_q[3])
    first, third = flip(first, 2), flip(third, 6)
    packed, *late, grad_q = call(
        weigh_kernel,
        jax.ShapeDtypeStruct((24, 128), f32),
        *[jax.ShapeDtypeStruct((16, 2176), f32)] * 4,
        jax.ShapeDtypeStruct((8, 2048), bf16),
    )(
        kept,
        flip(message, YH),
        sums,
        small,
        query,
        panel,
        p_all,
        gain_row,
        query_hidden,
        *pair_q,
        *near,
    )
    late = [late[0]] + [flip(late[s], 2 * s) for s in (1, 2, 3)]
    packed = packed + flip(packed, Z[2])
    packed, first, third, second, *late = tie(packed, first, third, pair_q[2], *late)
    second = flip(second, 4)
    own, give = call(
        late_kernel,
        jax.ShapeDtypeStruct((8, 2048), f32),
        jax.ShapeDtypeStruct((16, 2176), f32),
        scratch=[pltpu.VMEM((4, 16, 2176), f32), pltpu.SemaphoreType.DMA((4,))],
        limit=4,
        fetched=[False] + [True] * 4,
    )(slots, *late)
    got = flip(give, C)
    packed = packed + flip(packed, YH)
    packed, got = tie(packed, got)
    packed = packed + flip(packed, Z[1])
    packed, second = tie(packed, second)
    back = [pair_q[0], first, second, third]
    (other,) = call(
        pack_kernel,
        jax.ShapeDtypeStruct((192, 2048), bf16),
        scratch=[pltpu.VMEM((192, 2048), bf16), pltpu.SemaphoreType.DMA((4,))],
        limit=4,
        fetched=[True] * 4,
    )(*back)
    other = flip(other, C)
    packed = packed + flip(packed, Z[0])
    packed, other = tie(packed, other)
    grad_h, grad_p = call(
        hard_kernel,
        jax.ShapeDtypeStruct((512, 2048), bf16),
        jax.ShapeDtypeStruct((8, 2048), bf16),
        scratch=[
            pltpu.VMEM((512, 2048), bf16),
            pltpu.VMEM((512, 2048), bf16),
            pltpu.VMEM((8, 2048), f32),
            pltpu.VMEM((16, 2176), f32),
            pltpu.VMEM((16, 2176), f32),
            pltpu.SemaphoreType.DMA((15,)),
        ],
        limit=60,
        fetched=[True, False, False, False] + [True] * 8,
    )(hard_hidden, passage_hidden, gain_row, tot, own, give, got, *back, other)
    for mask in X:
        packed = packed + flip(packed, mask)
    packed, grad_h = tie(packed, grad_h)
    packed = packed + flip(packed, C)
    return grad_q, grad_p, grad_h, packed[:16].reshape(-1), packed[16, 0] / 1024


def solution(mesh):
    return jax.shard_map(
        local,
        mesh=mesh,
        in_specs=(
            P("dp", "mp"),
            P("dp", "mp"),
            P("dp", "mp"),
            P("mp"),
            P("dp", None, None),
            P("dp", None),
        ),
        out_specs=(P("dp", "mp"), P("dp", "mp"), P("dp", "mp"), P("mp"), P()),
        check_vma=False,
    )
```

```python
import functools

import jax
import jax.numpy as jnp
from jax import lax
from jax.experimental import pallas as pl
from jax.experimental.pallas import tpu as pltpu
from jax.sharding import PartitionSpec as P

D = 4096
normalizer_divisor = 0.02
eps_norm = 1e-06
f32 = jnp.float32
bf16 = jnp.bfloat16
C, X, Z, YH = 1, (2, 4), (8, 16, 32), 64
SWAP = [(0, 1), (1, 0)]


def flip(x, mask):
    return lax.ppermute(x, "dp", [(i, i ^ mask) for i in range(128)])


def double(x, mask):
    return jnp.concatenate([x, flip(x, mask)], 0)


def stats(values, gain):
    squares = values * values
    return jnp.sum(squares, axis=1), jnp.sum(squares * gain * gain, axis=1)


def scales(total_sq, total_gsq):
    scale = lax.rsqrt(total_sq / D + eps_norm)
    length = jnp.sqrt(scale * scale * total_gsq + eps_norm)
    return scale, length


def tie(*arrays):
    return lax.optimization_barrier(arrays)


def requests(hard_owner, hard_slot):
    owner = hard_owner.reshape(-1)
    slot = hard_slot.reshape(-1)
    number = jnp.arange(owner.shape[0], dtype=jnp.int32)
    earlier = (owner[:, None] == owner[None, :]) & (number[:, None] < number[None, :])
    position = jnp.sum(earlier.astype(jnp.int32), axis=0)
    low = slot % 256
    high = 1 + slot // 256 + 2 * (number // hard_slot.shape[1])
    place = jnp.arange(8, dtype=jnp.int32)[:, None]
    coded = jnp.where(
        place // 2 == position[None, :], jnp.where(place % 2 == 0, low[None, :], high[None, :]), 0
    ).astype(bf16)
    names = (owner[:, None] == jnp.arange(128, dtype=jnp.int32)[None, :]).astype(bf16)
    return jnp.dot(coded, names, preferred_element_type=f32).astype(bf16)


def diagonal(rows):
    shape = (rows, 128)
    return lax.broadcasted_iota(jnp.int32, shape, 0) == lax.broadcasted_iota(jnp.int32, shape, 1)


def as_row(column):
    return jnp.sum(jnp.where(diagonal(column.shape[0]), column, 0.0), axis=0, keepdims=True)


def as_column(row, rows):
    return jnp.sum(jnp.where(diagonal(rows), row, 0.0), axis=1, keepdims=True)


def all_passages(near):
    return jnp.concatenate([block[96:112] for block in near], 0)


def score_kernel(panel, gain, *refs):
    pair_q, near, out = refs[:4], refs[4:8], refs[8]
    g = gain[...]
    rows = panel[:, :2048]
    scaled = all_passages(near).astype(f32) * g
    high = scaled.astype(bf16)
    low = (scaled - high.astype(f32)).astype(bf16)
    contract = (((1,), (1,)), ((), ()))
    out[0:64] = lax.dot_general(
        high, rows, contract, preferred_element_type=f32
    ) + lax.dot_general(low, rows, contract, preferred_element_type=f32)
    values = rows.astype(f32)
    squares = values * values
    out[64:65] = as_row(jnp.sum(squares, axis=1, keepdims=True))
    out[65:66] = as_row(jnp.sum(squares * (g * g), axis=1, keepdims=True))
    for s in range(4):
        product = pair_q[s][...].astype(f32) * near[s][0:96].astype(f32) * g
        out[66 + s : 67 + s] = as_row(jnp.sum(product, axis=1, keepdims=True))
    out[70:72] = jnp.zeros((2, 128), f32)


def entry_columns(asked):
    row = lax.broadcasted_iota(jnp.int32, (96, 128), 0)
    entry = row >> 4
    entry = jnp.where(entry >= 3, 2 * entry - 5, 2 * entry)
    pick = (lax.broadcasted_iota(jnp.int32, (96, 128), 1) == (row & 15) * 8 + entry).astype(bf16)
    return jnp.dot(pick, asked, preferred_element_type=f32)


def decode(entries, column):
    lane = lax.broadcasted_iota(jnp.int32, (96, 128), 1)
    block = lax.broadcasted_iota(jnp.int32, (48, 1), 0) & 15
    values = jnp.sum(jnp.where(lane == column, entries, 0.0), axis=1, keepdims=True)
    low, high = values[:48].astype(jnp.int32), values[48:].astype(jnp.int32)
    slot = jnp.where(high > 0, low + 256 * ((high - 1) & 1), -1)
    return slot, jnp.where(high > 0, block * 8 + ((high - 1) >> 1), -1)


def row_of(index):
    return as_row((index + 1).astype(f32)).astype(jnp.int32) - 1


def one_hot(index, count):
    lanes = lax.broadcasted_iota(jnp.int32, (index.shape[0], count), 1)
    return (lanes == index).astype(f32)


def asker_kernel(me_ref, panel, *refs):
    pair_q, query = refs[:4], refs[4]
    me = me_ref[0]
    entries = entry_columns(panel[:, 2048:])
    for s in range(4):
        index = jnp.concatenate([decode(entries, me ^ (2 * s + t))[1] for t in range(2)], 0)
        query[s : s + 1] = row_of(index)
        pair_q[s][...] = jnp.dot(
            one_hot(index, 128).astype(bf16), panel[:, :2048], preferred_element_type=f32
        ).astype(bf16)
    query[4:8] = jnp.full((4, 128), -1, jnp.int32)


def owner_kernel(me_ref, panel, table_a, table_b, ratios, gain, p_a, p_b, *refs):
    half, rest, near, slots = refs[0], refs[1], refs[2:6], refs[6]
    me = me_ref[0]
    picks = ([], [])
    for s in range(4):
        asked = panel[:, 2048:]
        if s:
            part = slice(64 * s - 64, 64 * s)
            asked = jnp.concatenate([half[part], rest[part]], 0)
        entries = entry_columns(asked)
        both = [decode(entries, me ^ t)[0] for t in range(2)]
        for t in range(2):
            picks[t].append(one_hot(both[t], 512))
        slots[s : s + 1] = row_of(jnp.concatenate(both, 0))
    slots[4:8] = jnp.full((4, 128), -1, jnp.int32)
    for t, table in enumerate((table_a, table_b)):
        pick_h = jnp.concatenate(picks[t], 0)
        ratio = jnp.sum(jnp.where(pick_h > 0, ratios[t : t + 1], 0.0), axis=1, keepdims=True)
        values = jnp.dot(pick_h.astype(bf16), table[...], preferred_element_type=f32)
        values = (values * ratio * gain[...]).astype(bf16)
        for s in range(4):
            near[s][48 * t : 48 * t + 48] = values[48 * s : 48 * s + 48]
    both = jnp.concatenate([p_a[...].astype(f32), p_b[...].astype(f32)], 0).astype(bf16)
    for s in range(4):
        near[s][96:112] = both


def split_sums(v):
    high = v.astype(bf16).astype(f32)
    middle = (v - high).astype(bf16).astype(f32)
    parts = [high, middle, v - high - middle, jnp.zeros((10, 128), f32)]
    return jnp.concatenate(parts, 0).astype(bf16)


def swap_lanes(v, bits):
    lane = lax.broadcasted_iota(jnp.int32, (8, 128), 1)
    for bit in (8, 16, 32, 64):
        if bits & bit:
            v = jnp.where(
                (lane & bit) > 0, pltpu.roll(v, bit, axis=1), pltpu.roll(v, 128 - bit, axis=1)
            )
    return v


def add_kernel(kept, sums, *refs):
    got, out, message, out_sums = refs[:7], refs[7], refs[8], refs[9]
    total = kept[...]
    v = sums[...]
    zeros = jnp.zeros((6, 128), f32)
    for m in range(1, 8):
        block = got[m - 1][...].astype(f32)
        total = total + block[:, :2048]
        extra = block[:, 2048:]
        extra = jnp.concatenate([extra[0:2] + extra[2:4] + extra[4:6], zeros], 0)
        v = v + swap_lanes(extra, 16 * m)
    out[...] = total[:8]
    message[0:8] = total[8:]
    message[8:16, :128] = v
    message[8:16, 128:] = jnp.zeros((8, 1920), f32)
    out_sums[...] = v


def late_kernel(slots, *refs):
    arrived, own, give, late, done = refs[:4], refs[4], refs[5], refs[6], refs[7]
    copies = [pltpu.make_async_copy(arrived[s], late.at[s], done.at[s]) for s in range(4)]
    for copy in copies:
        copy.start()
    for copy in copies:
        copy.wait()
    own[...] = sum(late[s, 0:8, :2048] for s in range(4))
    give[0:8, :2048] = sum(late[s, 8:16, :2048] for s in range(4))
    give[8:16, :2048] = jnp.zeros((8, 2048), f32)
    for s in range(4):
        give[s : s + 1, 2048:] = late[s, 0:1, 2048:]
        give[4 + s : 5 + s, 2048:] = late[s, 1:2, 2048:]
    give[8:9, 2048:] = sum(late[s, 2:3, 2048:] for s in range(4))
    give[9:13, 2048:] = slots[0:4].astype(f32)
    give[13:16, 2048:] = jnp.zeros((3, 128), f32)


def pack_kernel(*refs):
    back, other, rows, done = refs[:4], refs[4], refs[5], refs[6]
    copies = [
        pltpu.make_async_copy(back[s].at[48:96], rows.at[48 * s : 48 * s + 48], done.at[s])
        for s in range(4)
    ]
    for copy in copies:
        copy.start()
    for copy in copies:
        copy.wait()
    other[...] = rows[...]


def finish(values, ratio, tail, g, grad, dot):
    return (ratio * g * (grad - values * ratio * g * dot) - values * (tail * dot)).astype(bf16)


def hard_kernel(hidden_ref, passages, gain, totals, own_ref, give_ref, got_ref, *refs):
    back, other, out, out_p = refs[:4], refs[4], refs[5], refs[6]
    rows, hidden, own, give, got, done = refs[7:]
    copies = [
        pltpu.make_async_copy(own_ref, own, done.at[8]),
        pltpu.make_async_copy(give_ref, give, done.at[9]),
        pltpu.make_async_copy(got_ref, got, done.at[10]),
    ]
    for s in range(4):
        first, second = rows.at[128 * s : 128 * s + 48], rows.at[128 * s + 48 : 128 * s + 96]
        copies.append(pltpu.make_async_copy(back[s].at[0:48], first, done.at[2 * s]))
        copies.append(
            pltpu.make_async_copy(other.at[48 * s : 48 * s + 48], second, done.at[2 * s + 1])
        )
    pieces = [
        pltpu.make_async_copy(
            hidden_ref.at[128 * i : 128 * i + 128],
            hidden.at[128 * i : 128 * i + 128],
            done.at[11 + i],
        )
        for i in range(4)
    ]
    for copy in copies + pieces:
        copy.start()
    for s in range(4):
        rows[128 * s + 96 : 128 * s + 128] = jnp.zeros((32, 2048), bf16)
    for copy in copies:
        copy.wait()
    g = gain[...]
    inverse = g / normalizer_divisor
    lane = lax.broadcasted_iota(jnp.int32, (16, 128), 1)
    facts = jnp.where(lane < 48, give[:, 2048:], got[:, 2048:])
    scale = lax.rsqrt(totals[0:1] / D + eps_norm)
    length = jnp.sqrt(scale * scale * totals[1:2] + eps_norm)
    ratio = scale / length
    tail = scale * scale * eps_norm / (length * length * D)
    slot = jnp.concatenate([facts[9 + s : 10 + s] for s in range(4)], 1).astype(jnp.int32)
    coeff = jnp.concatenate([facts[s : s + 1] for s in range(4)], 1)
    pair_dot = jnp.concatenate([facts[4 + s : 5 + s] for s in range(4)], 1)
    used = (lax.broadcasted_iota(jnp.int32, (1, 512), 1) & 127) < 96
    slot = jnp.where(used, slot, -1)
    for i in range(4):
        pick = lax.broadcasted_iota(jnp.int32, (128, 512), 0) + 128 * i == slot
        weights = jnp.where(pick, coeff, 0.0).astype(bf16)
        grad = jnp.dot(weights, rows[...], preferred_element_type=f32)
        dot = jnp.sum(jnp.where(pick, pair_dot, 0.0), axis=1, keepdims=True)
        part = slice(128 * i, 128 * i + 128)
        pieces[i].wait()
        values = hidden[part, :].astype(f32)
        ratio_part, tail_part = as_column(ratio[:, part], 128), as_column(tail[:, part], 128)
        out[part, :] = finish(values, ratio_part, tail_part, g, grad * inverse, dot)
    row = give[8:16, 2048:] + pltpu.roll(got[8:16, 2048:], 120, axis=1)
    dot = as_column(row[0:1], 8)
    grad = (own[...] + got[0:8, :2048]) * inverse
    out_p[...] = finish(
        passages[...].astype(f32),
        as_column(ratio[:, 512:640], 8),
        as_column(tail[:, 512:640], 8),
        g,
        grad,
        dot,
    )


def pull_kernel(part, got, query, *refs):
    near, kept, messages, sums, small = refs[:4], refs[4], refs[5:12], refs[12], refs[13]
    full = part[...] + got[...]
    scale = lax.rsqrt(full[64:65] / D + eps_norm)
    length = jnp.sqrt(scale * scale * full[65:66] + eps_norm)
    ratio = scale / length
    ratio_column = as_column(ratio, 128)
    s_in = full[:64] * ratio / normalizer_divisor
    e_in = jnp.exp(s_in)
    own = diagonal(64) & (lax.broadcasted_iota(jnp.int32, (64, 128), 0) < 8)
    total = lax.dot_general(
        jnp.where(own, 0.0, e_in).astype(bf16),
        all_passages(near),
        (((0,), (0,)), ((), ())),
        preferred_element_type=f32,
    )
    z = jnp.zeros((128, 1), f32)
    w = jnp.zeros((128, 1), f32)
    for s in range(4):
        asker = query[s : s + 1, :]
        pick = lax.broadcasted_iota(jnp.int32, (128, 128), 0) == asker
        ratio_pair = jnp.sum(jnp.where(pick, ratio_column, 0.0), axis=0, keepdims=True)
        s_pair = full[66 + s : 67 + s] * ratio_pair / normalizer_divisor
        e_pair = jnp.where(asker >= 0, jnp.exp(s_pair), 0.0)
        spread = jnp.where(pick, e_pair, 0.0)
        z = z + jnp.sum(spread, axis=1, keepdims=True)
        w = w + jnp.sum(spread * s_pair, axis=1, keepdims=True)
        total = total + jnp.dot(
            spread[:, :96].astype(bf16), near[s][0:96], preferred_element_type=f32
        )
        small[66 + s : 67 + s] = s_pair
        small[70 + s : 71 + s] = e_pair
        small[74 + s : 75 + s] = ratio_pair
    kept[...] = total[:16]
    small[0:64] = s_in
    z = jnp.sum(e_in, axis=0, keepdims=True) + as_row(z)
    w = jnp.sum(e_in * s_in, axis=0, keepdims=True) + as_row(w)
    v = jnp.concatenate([z, w], 0)
    extra = split_sums(v)
    for m in range(1, 8):
        messages[m - 1][:, :2048] = total[16 * m : 16 * m + 16].astype(bf16)
        messages[m - 1][:, 2048:] = extra
    sums[0:2] = v
    sums[2:8] = jnp.zeros((6, 128), f32)
    small[64:66] = v
    small[78:79] = scale
    small[79:80] = length


def weigh_kernel(kept, got, sums, small, query, panel, gain, own_ref, *refs):
    pair_q, near, packed, late, out_q = refs[:4], refs[4:8], refs[8], refs[9:13], refs[13]
    g = gain[...]
    pulled = kept[...] + got[0:8]
    total = sums[...] + swap_lanes(got[8:16, :128], 8)
    z, w = total[0:1], total[1:2]
    s_in = small[0:64]
    scale, length = small[78:79], small[79:80]
    ratio = scale / length
    own = diagonal(64) & (lax.broadcasted_iota(jnp.int32, (64, 128), 0) < 8)
    c_in = ((jnp.exp(s_in) / z - jnp.where(own, 1.0, 0.0)) * ratio).astype(bf16)
    grads = jnp.dot(c_in, panel[:, :2048], preferred_element_type=f32)
    dots = jnp.sum(c_in.astype(f32) * (s_in / ratio), axis=1, keepdims=True)
    z_column = as_column(z, 128)
    values = all_passages(near).astype(f32)
    p_own = values[0:8]
    first = jnp.sum(grads * values, axis=0, keepdims=True)
    second = jnp.sum(values * values * dots, axis=0, keepdims=True)
    for s in range(4):
        asker = query[s : s + 1, :]
        pick = lax.broadcasted_iota(jnp.int32, (128, 128), 0) == asker
        z_pair = jnp.sum(jnp.where(pick, z_column, 0.0), axis=0, keepdims=True)
        c_pair = jnp.where(asker >= 0, small[70 + s : 71 + s] / z_pair, 0.0)
        ratio_pair = small[74 + s : 75 + s]
        coeff = (c_pair * ratio_pair).astype(bf16).astype(f32)
        pair_dot = jnp.where(asker >= 0, coeff * small[66 + s : 67 + s] / ratio_pair, 0.0)
        h = near[s][0:96].astype(f32)
        first = first + jnp.sum(
            pair_q[s][...].astype(f32) * h * as_column(coeff, 96), axis=0, keepdims=True
        )
        second = second + jnp.sum(h * h * as_column(pair_dot, 96), axis=0, keepdims=True)
        late[s][:, :2048] = grads[16 * s : 16 * s + 16]
        late[s][0:1, 2048:] = coeff
        late[s][1:2, 2048:] = pair_dot
        late[s][2:3, 2048:] = as_row(dots[16 * s : 16 * s + 16])
        late[s][3:16, 2048:] = jnp.zeros((13, 128), f32)
    s_own = jnp.sum(jnp.where(own, s_in, 0.0), axis=0, keepdims=True)
    dot_own = as_column(w / z - s_own, 8)
    ratio_own = as_column(ratio, 8)
    values = own_ref[...].astype(f32)
    direct = values * ratio_own
    z_own = as_column(z, 8)
    excess = jnp.exp(as_column(s_own, 8)) / z_own - 1.0
    grad = (pulled / z_own + excess * p_own) / normalizer_divisor
    own_scale, own_length = as_column(scale, 8), as_column(length, 8)
    tail = own_scale * own_scale * eps_norm / (own_length * own_length * D)
    out_q[...] = finish(values, ratio_own, tail, g, grad, dot_own)
    third = jnp.sum(direct * direct * g * dot_own, axis=0, keepdims=True)
    result = first * (2.0 / normalizer_divisor) - second / g - third
    for i in range(16):
        packed[i : i + 1] = result[:, 128 * i : 128 * i + 128]
    lane = lax.broadcasted_iota(jnp.int32, (1, 128), 1)
    loss = jnp.sum(jnp.where(lane < 8, jnp.log(z) - s_own, 0.0), axis=1, keepdims=True)
    packed[16:24] = jnp.broadcast_to(loss, (8, 128))


def call(kernel, *shapes, scratch=(), limit=14, fetched=(), scalar=False):
    def run(*operands):
        spaces = [pltpu.HBM if own else pltpu.VMEM for own in fetched]
        spaces = spaces or [pltpu.SMEM if scalar and not i else pltpu.VMEM for i in range(len(operands))]
        return pl.pallas_call(
            kernel,
            out_shape=shapes,
            in_specs=[pl.BlockSpec(memory_space=space) for space in spaces],
            scratch_shapes=scratch,
            compiler_params=pltpu.CompilerParams(vmem_limit_bytes=limit * 1024 * 1024),
        )(*operands)

    return run


def local(query_hidden, passage_hidden, hard_hidden, gain, hard_owner, hard_slot):
    me = lax.axis_index("dp")
    p_vals = passage_hidden.astype(f32)
    h_vals = hard_hidden.astype(f32)
    p_sq, p_gsq = stats(p_vals, gain)
    h_sq, h_gsq = stats(h_vals, gain)
    mine = jnp.stack([jnp.concatenate([h_sq, p_sq]), jnp.concatenate([h_gsq, p_gsq])])
    mine = jnp.pad(mine, ((0, 0), (0, 120)))
    table = requests(hard_owner, hard_slot)
    panel = double(jnp.concatenate([query_hidden, table], 1), YH)
    panel, mine = tie(panel, mine)
    panel = double(panel, Z[2])
    tot = mine + lax.ppermute(mine, "mp", SWAP)
    panel, tot = tie(panel, tot)
    panel = double(panel, Z[1])
    scale, length = scales(tot[0], tot[1])
    p_scale, p_length = scale[512:520], length[512:520]
    h_scale, h_length = scale[:512], length[:512]
    p_emb = (p_vals * (p_scale / p_length)[:, None] * gain).astype(bf16)
    ratios = (h_scale / h_length)[None]
    panel, p_emb, hard_other = tie(panel, p_emb, flip(hard_hidden, C))
    half = jnp.concatenate([flip(panel[:, 2048:], 2 * s) for s in (1, 2, 3)], 0)
    rest = flip(half, Z[0])
    panel = double(panel, Z[0])
    p_other = flip(p_emb, C)
    ratios = jnp.concatenate([ratios, flip(ratios, C)], 0)
    panel, half, rest, p_other = tie(panel, half, rest, p_other)
    wide = jax.ShapeDtypeStruct((96, 2048), bf16)
    index = jax.ShapeDtypeStruct((8, 128), jnp.int32)
    *pair_q, query = call(asker_kernel, *[wide] * 4, index, scalar=True)(me[None], panel)
    deep = jax.ShapeDtypeStruct((112, 2048), bf16)
    *near, slots = call(owner_kernel, *[deep] * 4, index, scalar=True, limit=20)(
        me[None], panel, hard_hidden, hard_other, ratios, gain[None], p_emb, p_other, half, rest
    )
    near = [near[0]] + [flip(near[s], 2 * s) for s in (1, 2, 3)]
    gain_row = gain[None]

    (part,) = call(score_kernel, jax.ShapeDtypeStruct((72, 128), f32))(
        panel, gain_row, *pair_q, *near
    )
    got = lax.ppermute(part, "mp", SWAP)
    kept, *messages, sums, small = call(
        pull_kernel,
        jax.ShapeDtypeStruct((16, 2048), f32),
        *[jax.ShapeDtypeStruct((16, 2176), bf16)] * 7,
        jax.ShapeDtypeStruct((8, 128), f32),
        jax.ShapeDtypeStruct((80, 128), f32),
    )(part, got, query, *near)
    messages = [flip(message, mask) for message, mask in zip(messages, (32, 16, 48, 8, 40, 24, 56))]
    kept, message, sums = call(
        add_kernel,
        jax.ShapeDtypeStruct((8, 2048), f32),
        jax.ShapeDtypeStruct((16, 2048), f32),
        jax.ShapeDtypeStruct((8, 128), f32),
    )(kept, sums, *messages)
    kept, message, sums, first, third = tie(kept, message, sums, pair_q[1], pair_q[3])
    first, third = flip(first, 2), flip(third, 6)
    packed, *late, grad_q = call(
        weigh_kernel,
        jax.ShapeDtypeStruct((24, 128), f32),
        *[jax.ShapeDtypeStruct((16, 2176), f32)] * 4,
        jax.ShapeDtypeStruct((8, 2048), bf16),
    )(
        kept,
        flip(message, YH),
        sums,
        small,
        query,
        panel,
        gain_row,
        query_hidden,
        *pair_q,
        *near,
    )
    late = [late[0]] + [flip(late[s], 2 * s) for s in (1, 2, 3)]
    packed = packed + flip(packed, Z[2])
    packed, *late = tie(packed, *late)
    own, give = call(
        late_kernel,
        jax.ShapeDtypeStruct((8, 2048), f32),
        jax.ShapeDtypeStruct((16, 2176), f32),
        scratch=[pltpu.VMEM((4, 16, 2176), f32), pltpu.SemaphoreType.DMA((4,))],
        limit=4,
        fetched=[False] + [True] * 4,
    )(slots, *late)
    got = flip(give, C)
    packed = packed + flip(packed, YH)
    packed, got, first, third, second = tie(packed, got, first, third, pair_q[2])
    second = flip(second, 4)
    for mask in (Z[1], Z[0]):
        packed = packed + flip(packed, mask)
    packed, second = tie(packed, second)
    back = [pair_q[0], first, second, third]
    (other,) = call(
        pack_kernel,
        jax.ShapeDtypeStruct((192, 2048), bf16),
        scratch=[pltpu.VMEM((192, 2048), bf16), pltpu.SemaphoreType.DMA((4,))],
        limit=4,
        fetched=[True] * 4,
    )(*back)
    other = flip(other, C)
    packed = packed + flip(packed, X[0])
    packed, other = tie(packed, other)
    grad_h, grad_p = call(
        hard_kernel,
        jax.ShapeDtypeStruct((512, 2048), bf16),
        jax.ShapeDtypeStruct((8, 2048), bf16),
        scratch=[
            pltpu.VMEM((512, 2048), bf16),
            pltpu.VMEM((512, 2048), bf16),
            pltpu.VMEM((8, 2048), f32),
            pltpu.VMEM((16, 2176), f32),
            pltpu.VMEM((16, 2176), f32),
            pltpu.SemaphoreType.DMA((15,)),
        ],
        limit=60,
        fetched=[True, False, False, False] + [True] * 8,
    )(hard_hidden, passage_hidden, gain_row, tot, own, give, got, *back, other)
    packed = packed + flip(packed, X[1])
    packed, grad_h = tie(packed, grad_h)
    packed = packed + flip(packed, C)
    return grad_q, grad_p, grad_h, packed[:16].reshape(-1), packed[16, 0] / 1024


def solution(mesh):
    return jax.shard_map(
        local,
        mesh=mesh,
        in_specs=(
            P("dp", "mp"),
            P("dp", "mp"),
            P("dp", "mp"),
            P("mp"),
            P("dp", None, None),
            P("dp", None),
        ),
        out_specs=(P("dp", "mp"), P("dp", "mp"), P("dp", "mp"), P("mp"), P()),
        check_vma=False,
    )
```

```python
import functools

import jax
import jax.numpy as jnp
from jax import lax
from jax.experimental import pallas as pl
from jax.experimental.pallas import tpu as pltpu
from jax.sharding import PartitionSpec as P

D = 4096
normalizer_divisor = 0.02
eps_norm = 1e-06
f32 = jnp.float32
bf16 = jnp.bfloat16
C, X, Z, YH = 1, (2, 4), (8, 16, 32), 64
SWAP = [(0, 1), (1, 0)]


def flip(x, mask):
    return lax.ppermute(x, "dp", [(i, i ^ mask) for i in range(128)])


def double(x, mask):
    return jnp.concatenate([x, flip(x, mask)], 0)


def stats(values, gain):
    squares = values * values
    return jnp.sum(squares, axis=1), jnp.sum(squares * gain * gain, axis=1)


def scales(total_sq, total_gsq):
    scale = lax.rsqrt(total_sq / D + eps_norm)
    length = jnp.sqrt(scale * scale * total_gsq + eps_norm)
    return scale, length


def tie(*arrays):
    return lax.optimization_barrier(arrays)


def requests(hard_owner, hard_slot):
    owner = hard_owner.reshape(-1)
    slot = hard_slot.reshape(-1)
    number = jnp.arange(owner.shape[0], dtype=jnp.int32)
    earlier = (owner[:, None] == owner[None, :]) & (number[:, None] < number[None, :])
    position = jnp.sum(earlier.astype(jnp.int32), axis=0)
    low = slot % 256
    high = 1 + slot // 256 + 2 * (number // hard_slot.shape[1])
    place = jnp.arange(8, dtype=jnp.int32)[:, None]
    coded = jnp.where(
        place // 2 == position[None, :], jnp.where(place % 2 == 0, low[None, :], high[None, :]), 0
    ).astype(bf16)
    names = (owner[:, None] == jnp.arange(128, dtype=jnp.int32)[None, :]).astype(bf16)
    return jnp.dot(coded, names, preferred_element_type=f32).astype(bf16)


def diagonal(rows):
    shape = (rows, 128)
    return lax.broadcasted_iota(jnp.int32, shape, 0) == lax.broadcasted_iota(jnp.int32, shape, 1)


def as_row(column):
    return jnp.sum(jnp.where(diagonal(column.shape[0]), column, 0.0), axis=0, keepdims=True)


def as_column(row, rows):
    return jnp.sum(jnp.where(diagonal(rows), row, 0.0), axis=1, keepdims=True)


def all_passages(near):
    return jnp.concatenate([block[96:112] for block in near], 0)


def score_kernel(panel, gain, *refs):
    pair_q, near, out = refs[:4], refs[4:8], refs[8]
    g = gain[...]
    rows = panel[:, :2048]
    scaled = all_passages(near).astype(f32) * g
    high = scaled.astype(bf16)
    low = (scaled - high.astype(f32)).astype(bf16)
    contract = (((1,), (1,)), ((), ()))
    out[0:64] = lax.dot_general(
        high, rows, contract, preferred_element_type=f32
    ) + lax.dot_general(low, rows, contract, preferred_element_type=f32)
    values = rows.astype(f32)
    squares = values * values
    out[64:65] = as_row(jnp.sum(squares, axis=1, keepdims=True))
    out[65:66] = as_row(jnp.sum(squares * (g * g), axis=1, keepdims=True))
    for s in range(4):
        product = pair_q[s][...].astype(f32) * near[s][0:96].astype(f32) * g
        out[66 + s : 67 + s] = as_row(jnp.sum(product, axis=1, keepdims=True))
    out[70:72] = jnp.zeros((2, 128), f32)


def entry_columns(asked):
    row = lax.broadcasted_iota(jnp.int32, (96, 128), 0)
    entry = row >> 4
    entry = jnp.where(entry >= 3, 2 * entry - 5, 2 * entry)
    pick = (lax.broadcasted_iota(jnp.int32, (96, 128), 1) == (row & 15) * 8 + entry).astype(bf16)
    return jnp.dot(pick, asked, preferred_element_type=f32)


def decode(entries, column):
    lane = lax.broadcasted_iota(jnp.int32, (96, 128), 1)
    block = lax.broadcasted_iota(jnp.int32, (48, 1), 0) & 15
    values = jnp.sum(jnp.where(lane == column, entries, 0.0), axis=1, keepdims=True)
    low, high = values[:48].astype(jnp.int32), values[48:].astype(jnp.int32)
    slot = jnp.where(high > 0, low + 256 * ((high - 1) & 1), -1)
    return slot, jnp.where(high > 0, block * 8 + ((high - 1) >> 1), -1)


def row_of(index):
    return as_row((index + 1).astype(f32)).astype(jnp.int32) - 1


def one_hot(index, count):
    lanes = lax.broadcasted_iota(jnp.int32, (index.shape[0], count), 1)
    return (lanes == index).astype(f32)


def asker_kernel(me_ref, panel, *refs):
    pair_q, query = refs[:4], refs[4]
    me = me_ref[0]
    entries = entry_columns(panel[:, 2048:])
    for s in range(4):
        index = jnp.concatenate([decode(entries, me ^ (2 * s + t))[1] for t in range(2)], 0)
        query[s : s + 1] = row_of(index)
        pair_q[s][...] = jnp.dot(
            one_hot(index, 128).astype(bf16), panel[:, :2048], preferred_element_type=f32
        ).astype(bf16)
    query[4:8] = jnp.full((4, 128), -1, jnp.int32)


def owner_kernel(me_ref, panel, table_a, table_b, ratios, gain, p_a, p_b, *refs):
    half, rest, near, slots = refs[0], refs[1], refs[2:6], refs[6]
    me = me_ref[0]
    picks = ([], [])
    for s in range(4):
        asked = panel[:, 2048:]
        if s:
            part = slice(64 * s - 64, 64 * s)
            asked = jnp.concatenate([half[part], rest[part]], 0)
        entries = entry_columns(asked)
        both = [decode(entries, me ^ t)[0] for t in range(2)]
        for t in range(2):
            picks[t].append(one_hot(both[t], 512))
        slots[s : s + 1] = row_of(jnp.concatenate(both, 0))
    slots[4:8] = jnp.full((4, 128), -1, jnp.int32)
    for t, table in enumerate((table_a, table_b)):
        pick_h = jnp.concatenate(picks[t], 0)
        ratio = jnp.sum(jnp.where(pick_h > 0, ratios[t : t + 1], 0.0), axis=1, keepdims=True)
        values = jnp.dot(pick_h.astype(bf16), table[...], preferred_element_type=f32)
        values = (values * ratio * gain[...]).astype(bf16)
        for s in range(4):
            near[s][48 * t : 48 * t + 48] = values[48 * s : 48 * s + 48]
    both = jnp.concatenate([p_a[...].astype(f32), p_b[...].astype(f32)], 0).astype(bf16)
    for s in range(4):
        near[s][96:112] = both


def split_sums(v):
    high = v.astype(bf16).astype(f32)
    middle = (v - high).astype(bf16).astype(f32)
    parts = [high, middle, v - high - middle, jnp.zeros((10, 128), f32)]
    return jnp.concatenate(parts, 0).astype(bf16)


def swap_lanes(v, bits):
    lane = lax.broadcasted_iota(jnp.int32, (8, 128), 1)
    for bit in (8, 16, 32, 64):
        if bits & bit:
            v = jnp.where(
                (lane & bit) > 0, pltpu.roll(v, bit, axis=1), pltpu.roll(v, 128 - bit, axis=1)
            )
    return v


def add_kernel(kept, sums, *refs):
    got, out, message, out_sums = refs[:7], refs[7], refs[8], refs[9]
    total = kept[...]
    v = sums[...]
    zeros = jnp.zeros((6, 128), f32)
    for m in range(1, 8):
        block = got[m - 1][...].astype(f32)
        total = total + block[:, :2048]
        extra = block[:, 2048:]
        extra = jnp.concatenate([extra[0:2] + extra[2:4] + extra[4:6], zeros], 0)
        v = v + swap_lanes(extra, 16 * m)
    out[...] = total[:8]
    message[0:8] = total[8:]
    message[8:16, :128] = v
    message[8:16, 128:] = jnp.zeros((8, 1920), f32)
    out_sums[...] = v


def late_kernel(slots, *refs):
    arrived, own, give, late, done = refs[:4], refs[4], refs[5], refs[6], refs[7]
    copies = [pltpu.make_async_copy(arrived[s], late.at[s], done.at[s]) for s in range(4)]
    for copy in copies:
        copy.start()
    for copy in copies:
        copy.wait()
    own[...] = sum(late[s, 0:8, :2048] for s in range(4))
    give[0:8, :2048] = sum(late[s, 8:16, :2048] for s in range(4))
    give[8:16, :2048] = jnp.zeros((8, 2048), f32)
    for s in range(4):
        give[s : s + 1, 2048:] = late[s, 0:1, 2048:]
        give[4 + s : 5 + s, 2048:] = late[s, 1:2, 2048:]
    give[8:9, 2048:] = sum(late[s, 2:3, 2048:] for s in range(4))
    give[9:13, 2048:] = slots[0:4].astype(f32)
    give[13:16, 2048:] = jnp.zeros((3, 128), f32)


def pack_kernel(*refs):
    back, other, rows, done = refs[:4], refs[4], refs[5], refs[6]
    copies = [
        pltpu.make_async_copy(back[s].at[48:96], rows.at[48 * s : 48 * s + 48], done.at[s])
        for s in range(4)
    ]
    for copy in copies:
        copy.start()
    for copy in copies:
        copy.wait()
    other[...] = rows[...]


def finish(values, ratio, tail, g, grad, dot):
    return (ratio * g * (grad - values * ratio * g * dot) - values * (tail * dot)).astype(bf16)


def hard_kernel(hidden_ref, passages, gain, totals, own_ref, give_ref, got_ref, *refs):
    back, other, out, out_p = refs[:4], refs[4], refs[5], refs[6]
    rows, hidden, own, give, got, done = refs[7:]
    copies = [
        pltpu.make_async_copy(own_ref, own, done.at[8]),
        pltpu.make_async_copy(give_ref, give, done.at[9]),
        pltpu.make_async_copy(got_ref, got, done.at[10]),
    ]
    for s in range(4):
        first, second = rows.at[128 * s : 128 * s + 48], rows.at[128 * s + 48 : 128 * s + 96]
        copies.append(pltpu.make_async_copy(back[s].at[0:48], first, done.at[2 * s]))
        copies.append(
            pltpu.make_async_copy(other.at[48 * s : 48 * s + 48], second, done.at[2 * s + 1])
        )
    pieces = [
        pltpu.make_async_copy(
            hidden_ref.at[128 * i : 128 * i + 128],
            hidden.at[128 * i : 128 * i + 128],
            done.at[11 + i],
        )
        for i in range(4)
    ]
    for copy in copies + pieces:
        copy.start()
    for s in range(4):
        rows[128 * s + 96 : 128 * s + 128] = jnp.zeros((32, 2048), bf16)
    for copy in copies:
        copy.wait()
    g = gain[...]
    inverse = g / normalizer_divisor
    lane = lax.broadcasted_iota(jnp.int32, (16, 128), 1)
    facts = jnp.where(lane < 48, give[:, 2048:], got[:, 2048:])
    scale = lax.rsqrt(totals[0:1] / D + eps_norm)
    length = jnp.sqrt(scale * scale * totals[1:2] + eps_norm)
    ratio = scale / length
    tail = scale * scale * eps_norm / (length * length * D)
    slot = jnp.concatenate([facts[9 + s : 10 + s] for s in range(4)], 1).astype(jnp.int32)
    coeff = jnp.concatenate([facts[s : s + 1] for s in range(4)], 1)
    pair_dot = jnp.concatenate([facts[4 + s : 5 + s] for s in range(4)], 1)
    used = (lax.broadcasted_iota(jnp.int32, (1, 512), 1) & 127) < 96
    slot = jnp.where(used, slot, -1)
    for i in range(4):
        pick = lax.broadcasted_iota(jnp.int32, (128, 512), 0) + 128 * i == slot
        weights = jnp.where(pick, coeff, 0.0).astype(bf16)
        grad = jnp.dot(weights, rows[...], preferred_element_type=f32)
        dot = jnp.sum(jnp.where(pick, pair_dot, 0.0), axis=1, keepdims=True)
        part = slice(128 * i, 128 * i + 128)
        pieces[i].wait()
        values = hidden[part, :].astype(f32)
        ratio_part, tail_part = as_column(ratio[:, part], 128), as_column(tail[:, part], 128)
        out[part, :] = finish(values, ratio_part, tail_part, g, grad * inverse, dot)
    row = give[8:16, 2048:] + pltpu.roll(got[8:16, 2048:], 120, axis=1)
    dot = as_column(row[0:1], 8)
    grad = (own[...] + got[0:8, :2048]) * inverse
    out_p[...] = finish(
        passages[...].astype(f32),
        as_column(ratio[:, 512:640], 8),
        as_column(tail[:, 512:640], 8),
        g,
        grad,
        dot,
    )


def pull_kernel(part, got, query, *refs):
    near, kept, messages, sums, small = refs[:4], refs[4], refs[5:12], refs[12], refs[13]
    full = part[...] + got[...]
    scale = lax.rsqrt(full[64:65] / D + eps_norm)
    length = jnp.sqrt(scale * scale * full[65:66] + eps_norm)
    ratio = scale / length
    ratio_column = as_column(ratio, 128)
    s_in = full[:64] * ratio / normalizer_divisor
    e_in = jnp.exp(s_in)
    own = diagonal(64) & (lax.broadcasted_iota(jnp.int32, (64, 128), 0) < 8)
    total = lax.dot_general(
        jnp.where(own, 0.0, e_in).astype(bf16),
        all_passages(near),
        (((0,), (0,)), ((), ())),
        preferred_element_type=f32,
    )
    z = jnp.zeros((128, 1), f32)
    w = jnp.zeros((128, 1), f32)
    for s in range(4):
        asker = query[s : s + 1, :]
        pick = lax.broadcasted_iota(jnp.int32, (128, 128), 0) == asker
        ratio_pair = jnp.sum(jnp.where(pick, ratio_column, 0.0), axis=0, keepdims=True)
        s_pair = full[66 + s : 67 + s] * ratio_pair / normalizer_divisor
        e_pair = jnp.where(asker >= 0, jnp.exp(s_pair), 0.0)
        spread = jnp.where(pick, e_pair, 0.0)
        z = z + jnp.sum(spread, axis=1, keepdims=True)
        w = w + jnp.sum(spread * s_pair, axis=1, keepdims=True)
        total = total + jnp.dot(
            spread[:, :96].astype(bf16), near[s][0:96], preferred_element_type=f32
        )
        small[66 + s : 67 + s] = s_pair
        small[70 + s : 71 + s] = e_pair
        small[74 + s : 75 + s] = ratio_pair
    kept[...] = total[:16]
    small[0:64] = s_in
    z = jnp.sum(e_in, axis=0, keepdims=True) + as_row(z)
    w = jnp.sum(e_in * s_in, axis=0, keepdims=True) + as_row(w)
    v = jnp.concatenate([z, w], 0)
    extra = split_sums(v)
    for m in range(1, 8):
        messages[m - 1][:, :2048] = total[16 * m : 16 * m + 16].astype(bf16)
        messages[m - 1][:, 2048:] = extra
    sums[0:2] = v
    sums[2:8] = jnp.zeros((6, 128), f32)
    small[64:66] = v
    small[78:79] = scale
    small[79:80] = length


def weigh_kernel(kept, got, sums, small, query, panel, gain, own_ref, *refs):
    pair_q, near, packed, late, out_q = refs[:4], refs[4:8], refs[8], refs[9:13], refs[13]
    g = gain[...]
    pulled = kept[...] + got[0:8]
    total = sums[...] + swap_lanes(got[8:16, :128], 8)
    z, w = total[0:1], total[1:2]
    s_in = small[0:64]
    scale, length = small[78:79], small[79:80]
    ratio = scale / length
    own = diagonal(64) & (lax.broadcasted_iota(jnp.int32, (64, 128), 0) < 8)
    c_in = ((jnp.exp(s_in) / z - jnp.where(own, 1.0, 0.0)) * ratio).astype(bf16)
    grads = jnp.dot(c_in, panel[:, :2048], preferred_element_type=f32)
    dots = jnp.sum(c_in.astype(f32) * (s_in / ratio), axis=1, keepdims=True)
    z_column = as_column(z, 128)
    values = all_passages(near).astype(f32)
    p_own = values[0:8]
    first = jnp.sum(grads * values, axis=0, keepdims=True)
    second = jnp.sum(values * values * dots, axis=0, keepdims=True)
    for s in range(4):
        asker = query[s : s + 1, :]
        pick = lax.broadcasted_iota(jnp.int32, (128, 128), 0) == asker
        z_pair = jnp.sum(jnp.where(pick, z_column, 0.0), axis=0, keepdims=True)
        c_pair = jnp.where(asker >= 0, small[70 + s : 71 + s] / z_pair, 0.0)
        ratio_pair = small[74 + s : 75 + s]
        coeff = (c_pair * ratio_pair).astype(bf16).astype(f32)
        pair_dot = jnp.where(asker >= 0, coeff * small[66 + s : 67 + s] / ratio_pair, 0.0)
        h = near[s][0:96].astype(f32)
        first = first + jnp.sum(
            pair_q[s][...].astype(f32) * h * as_column(coeff, 96), axis=0, keepdims=True
        )
        second = second + jnp.sum(h * h * as_column(pair_dot, 96), axis=0, keepdims=True)
        late[s][:, :2048] = grads[16 * s : 16 * s + 16]
        late[s][0:1, 2048:] = coeff
        late[s][1:2, 2048:] = pair_dot
        late[s][2:3, 2048:] = as_row(dots[16 * s : 16 * s + 16])
        late[s][3:16, 2048:] = jnp.zeros((13, 128), f32)
    s_own = jnp.sum(jnp.where(own, s_in, 0.0), axis=0, keepdims=True)
    dot_own = as_column(w / z - s_own, 8)
    ratio_own = as_column(ratio, 8)
    values = own_ref[...].astype(f32)
    direct = values * ratio_own
    z_own = as_column(z, 8)
    excess = jnp.exp(as_column(s_own, 8)) / z_own - 1.0
    grad = (pulled / z_own + excess * p_own) / normalizer_divisor
    own_scale, own_length = as_column(scale, 8), as_column(length, 8)
    tail = own_scale * own_scale * eps_norm / (own_length * own_length * D)
    out_q[...] = finish(values, ratio_own, tail, g, grad, dot_own)
    third = jnp.sum(direct * direct * g * dot_own, axis=0, keepdims=True)
    result = first * (2.0 / normalizer_divisor) - second / g - third
    for i in range(16):
        packed[i : i + 1] = result[:, 128 * i : 128 * i + 128]
    lane = lax.broadcasted_iota(jnp.int32, (1, 128), 1)
    loss = jnp.sum(jnp.where(lane < 8, jnp.log(z) - s_own, 0.0), axis=1, keepdims=True)
    packed[16:24] = jnp.broadcast_to(loss, (8, 128))


def call(kernel, *shapes, scratch=(), limit=14, fetched=(), scalar=False):
    def run(*operands):
        spaces = [pltpu.HBM if own else pltpu.VMEM for own in fetched]
        spaces = spaces or [pltpu.SMEM if scalar and not i else pltpu.VMEM for i in range(len(operands))]
        return pl.pallas_call(
            kernel,
            out_shape=shapes,
            in_specs=[pl.BlockSpec(memory_space=space) for space in spaces],
            scratch_shapes=scratch,
            compiler_params=pltpu.CompilerParams(vmem_limit_bytes=limit * 1024 * 1024),
        )(*operands)

    return run


def local(query_hidden, passage_hidden, hard_hidden, gain, hard_owner, hard_slot):
    me = lax.axis_index("dp")
    p_vals = passage_hidden.astype(f32)
    h_vals = hard_hidden.astype(f32)
    p_sq, p_gsq = stats(p_vals, gain)
    h_sq, h_gsq = stats(h_vals, gain)
    mine = jnp.stack([jnp.concatenate([h_sq, p_sq]), jnp.concatenate([h_gsq, p_gsq])])
    mine = jnp.pad(mine, ((0, 0), (0, 120)))
    table = requests(hard_owner, hard_slot)
    panel = double(jnp.concatenate([query_hidden, table], 1), YH)
    panel, mine = tie(panel, mine)
    panel = double(panel, Z[2])
    tot = mine + lax.ppermute(mine, "mp", SWAP)
    panel, tot = tie(panel, tot)
    panel = double(panel, Z[1])
    scale, length = scales(tot[0], tot[1])
    p_scale, p_length = scale[512:520], length[512:520]
    h_scale, h_length = scale[:512], length[:512]
    p_emb = (p_vals * (p_scale / p_length)[:, None] * gain).astype(bf16)
    ratios = (h_scale / h_length)[None]
    panel, p_emb, hard_other = tie(panel, p_emb, flip(hard_hidden, C))
    half = jnp.concatenate([flip(panel[:, 2048:], 2 * s) for s in (1, 2, 3)], 0)
    rest = flip(half, Z[0])
    panel = double(panel, Z[0])
    p_other = flip(p_emb, C)
    ratios = jnp.concatenate([ratios, flip(ratios, C)], 0)
    panel, half, rest, p_other = tie(panel, half, rest, p_other)
    wide = jax.ShapeDtypeStruct((96, 2048), bf16)
    index = jax.ShapeDtypeStruct((8, 128), jnp.int32)
    *pair_q, query = call(asker_kernel, *[wide] * 4, index, scalar=True)(me[None], panel)
    deep = jax.ShapeDtypeStruct((112, 2048), bf16)
    *near, slots = call(owner_kernel, *[deep] * 4, index, scalar=True, limit=20)(
        me[None], panel, hard_hidden, hard_other, ratios, gain[None], p_emb, p_other, half, rest
    )
    near = [near[0]] + [flip(near[s], 2 * s) for s in (1, 2, 3)]
    gain_row = gain[None]

    (part,) = call(score_kernel, jax.ShapeDtypeStruct((72, 128), f32))(
        panel, gain_row, *pair_q, *near
    )
    got = lax.ppermute(part, "mp", SWAP)
    kept, *messages, sums, small = call(
        pull_kernel,
        jax.ShapeDtypeStruct((16, 2048), f32),
        *[jax.ShapeDtypeStruct((16, 2176), bf16)] * 7,
        jax.ShapeDtypeStruct((8, 128), f32),
        jax.ShapeDtypeStruct((80, 128), f32),
    )(part, got, query, *near)
    messages = [flip(message, mask) for message, mask in zip(messages, (32, 16, 48, 8, 40, 24, 56))]
    kept, message, sums = call(
        add_kernel,
        jax.ShapeDtypeStruct((8, 2048), f32),
        jax.ShapeDtypeStruct((16, 2048), f32),
        jax.ShapeDtypeStruct((8, 128), f32),
    )(kept, sums, *messages)
    kept, message, sums, first, third = tie(kept, message, sums, pair_q[1], pair_q[3])
    first, third = flip(first, 2), flip(third, 6)
    packed, *late, grad_q = call(
        weigh_kernel,
        jax.ShapeDtypeStruct((24, 128), f32),
        *[jax.ShapeDtypeStruct((16, 2176), f32)] * 4,
        jax.ShapeDtypeStruct((8, 2048), bf16),
    )(
        kept,
        flip(message, YH),
        sums,
        small,
        query,
        panel,
        gain_row,
        query_hidden,
        *pair_q,
        *near,
    )
    late = [late[0]] + [flip(late[s], 2 * s) for s in (1, 2, 3)]
    packed = packed + flip(packed, Z[2])
    packed, second, *late = tie(packed, pair_q[2], *late)
    second = flip(second, 4)
    own, give = call(
        late_kernel,
        jax.ShapeDtypeStruct((8, 2048), f32),
        jax.ShapeDtypeStruct((16, 2176), f32),
        scratch=[pltpu.VMEM((4, 16, 2176), f32), pltpu.SemaphoreType.DMA((4,))],
        limit=4,
        fetched=[False] + [True] * 4,
    )(slots, *late)
    got = flip(give, C)
    packed = packed + flip(packed, YH)
    packed, got, first, third = tie(packed, got, first, third)
    for mask in (Z[1], Z[0]):
        packed = packed + flip(packed, mask)
    packed, second = tie(packed, second)
    back = [pair_q[0], first, second, third]
    (other,) = call(
        pack_kernel,
        jax.ShapeDtypeStruct((192, 2048), bf16),
        scratch=[pltpu.VMEM((192, 2048), bf16), pltpu.SemaphoreType.DMA((4,))],
        limit=4,
        fetched=[True] * 4,
    )(*back)
    other = flip(other, C)
    packed = packed + flip(packed, X[0])
    packed, other = tie(packed, other)
    grad_h, grad_p = call(
        hard_kernel,
        jax.ShapeDtypeStruct((512, 2048), bf16),
        jax.ShapeDtypeStruct((8, 2048), bf16),
        scratch=[
            pltpu.VMEM((512, 2048), bf16),
            pltpu.VMEM((512, 2048), bf16),
            pltpu.VMEM((8, 2048), f32),
            pltpu.VMEM((16, 2176), f32),
            pltpu.VMEM((16, 2176), f32),
            pltpu.SemaphoreType.DMA((15,)),
        ],
        limit=60,
        fetched=[True, False, False, False] + [True] * 8,
    )(hard_hidden, passage_hidden, gain_row, tot, own, give, got, *back, other)
    packed = packed + flip(packed, X[1])
    packed, grad_h = tie(packed, grad_h)
    packed = packed + flip(packed, C)
    return grad_q, grad_p, grad_h, packed[:16].reshape(-1), packed[16, 0] / 1024


def solution(mesh):
    return jax.shard_map(
        local,
        mesh=mesh,
        in_specs=(
            P("dp", "mp"),
            P("dp", "mp"),
            P("dp", "mp"),
            P("mp"),
            P("dp", None, None),
            P("dp", None),
        ),
        out_specs=(P("dp", "mp"), P("dp", "mp"), P("dp", "mp"), P("mp"), P()),
        check_vma=False,
    )
```
